32 devices in a mesh: band: 16 (over z, y, x), sample: 2 (over core).
Axes of the slice: x: 2, y: 2, z: 4, core: 2. Of those that a mesh axis runs over, the one named last changes fastest.
Arguments:
- features: bfloat16 [80, 768, 1024], P('band', 'sample'), may hold values from 0 to 20
- w_point: bfloat16 [1024, 256], replicated, may hold values from -0.1875 to 0.1875
- w_atrous: bfloat16 [3, 3, 3, 1024, 256], replicated, may hold values from -0.0625 to 0.0625
- w_pool: bfloat16 [1024, 256], replicated, may hold values from -0.1875 to 0.1875
- branch_gain: float32 [5, 256], replicated, may hold values from 0.1 to 1.9
- branch_bias: float32 [5, 256], replicated, may hold values from -3 to 3
- w_project: bfloat16 [1280, 256], replicated, may hold values from -0.15625 to 0.15625
- project_gain: float32 [256], replicated, may hold values from 0.1 to 1.9
- project_bias: float32 [256], replicated, may hold values from -3 to 3
- pixel_order: int32 [80, 768], P('band', 'sample'), may hold values from 0 to 1919, as said below
Outputs:
- owned: bfloat16 [61440, 256], P(('band', 'sample'))
The draws below stay inside these ranges and needn't reach their ends.
Inputs may be any that keep to these rules, and one draw needn't show every extreme that they name: `pixel_order`: within the 5 x 384 cells of one block of rows b * 5 to (b + 1) * 5 - 1 and columns h * 384 to (h + 1) * 384 - 1, the values are a permutation of 0 to 1919, each naming a cell of that block counted row by row.
All inputs are finite; a program needn't handle non-finite values.
Results may differ from the reference program's by a relative error of at most 0.0051.
Values may be sent and summed in bfloat16 or wider, within the bound.
No kernel may reach another device: no remote copies, remote signals or barrier semaphores. Data moves between devices by JAX's collectives and lax.ppermute only.
A program may use at most 192 MiB of HBM per device.

```python
import jax
import jax.numpy as jnp

C_IN = 1024
ASPP = 256
ROW_DEV = 5
W = 768
W_DEV = 384
ROWS = 80


def draw_features(key, part):
    base_key, column_key = jax.random.split(key)
    shape = (ROWS, W, C_IN)
    latitude = jnp.arange(ROWS, dtype=jnp.float32)[:, None, None] / ROWS
    column_scale = 10.0 ** (jax.random.uniform(column_key, (1, W, 1), jnp.float32) - 0.5)
    base = 2.0 * jax.random.uniform(base_key, shape, jnp.float32)
    row_scale = 10.0 ** (latitude - 0.5)
    return (base * row_scale * column_scale).astype(jnp.bfloat16)


def draw_pixel_order(key, part):
    band_count = ROWS // ROW_DEV
    half_count = W // W_DEV
    block_keys = jax.random.split(key, band_count * half_count)
    orders = jax.vmap(lambda block_key: jax.random.permutation(block_key, ROW_DEV * W_DEV))(block_keys)
    orders = orders.reshape(band_count, half_count, ROW_DEV, W_DEV)
    orders = jnp.transpose(orders, (0, 2, 1, 3))
    return orders.reshape(ROWS, W).astype(jnp.int32)


def scatter_about(own_key, extent, scale, limit, held_as=jnp.bfloat16):
    return jnp.clip(scale * jax.random.normal(own_key, extent, jnp.float32), -limit, limit).astype(held_as)


def setup_inputs(seed: int = 0) -> dict:
    keys = jax.random.split(jax.random.key(seed), 11)
    features = draw_features(jax.random.fold_in(keys[10], 71), 0)
    w_point = scatter_about(keys[1], (C_IN, ASPP), C_IN ** -0.5, 0.1875)
    w_atrous = scatter_about(keys[2], (3, 3, 3, C_IN, ASPP), (9 * C_IN) ** -0.5, 0.0625)
    w_pool = scatter_about(keys[3], (C_IN, ASPP), C_IN ** -0.5, 0.1875)
    branch_gain = jnp.clip(1.0 + 0.18 * jax.random.normal(keys[4], (5, ASPP), jnp.float32), 0.1, 1.9)
    branch_bias = scatter_about(keys[5], (5, ASPP), 0.5, 3.0, jnp.float32)
    w_project = scatter_about(keys[6], (5 * ASPP, ASPP), (5 * ASPP) ** -0.5, 0.15625)
    project_gain = jnp.clip(1.0 + 0.18 * jax.random.normal(keys[7], (ASPP,), jnp.float32), 0.1, 1.9)
    project_bias = scatter_about(keys[8], (ASPP,), 0.5, 3.0, jnp.float32)
    pixel_order = draw_pixel_order(jax.random.fold_in(keys[10], 71), 0)
    return dict(features=features, w_point=w_point, w_atrous=w_atrous, w_pool=w_pool, branch_gain=branch_gain, branch_bias=branch_bias, w_project=w_project, project_gain=project_gain, project_bias=project_bias, pixel_order=pixel_order)


dilation_list = (12, 24, 36)


def offset_rows(field, offset):
    row_count = field.shape[0]
    if offset == 0:
        return field
    padding = jnp.zeros((abs(offset),) + field.shape[1:], field.dtype)
    if offset > 0:
        return jnp.concatenate([field[offset:], padding], axis=0)[:row_count]
    keep_count = max(row_count + offset, 0)
    return jnp.concatenate([padding, field[:keep_count]], axis=0)[:row_count]


def activate(values, gain, shift_term):
    return jnp.maximum(values * gain + shift_term, 0.0).astype(jnp.bfloat16)


def whole_map(feature_map, w_point, w_atrous, w_pool, branch_gain, branch_bias, w_project, project_gain, project_bias):
    height, width_cells, channels = feature_map.shape
    totals = jnp.sum(feature_map.astype(jnp.float32), axis=(0, 1))
    pooled = totals / (height * width_cells)
    pool_input = pooled.astype(jnp.bfloat16)
    pool_value = jnp.dot(pool_input[None, :], w_pool, preferred_element_type=jnp.float32)[0]
    pool_branch = activate(pool_value, branch_gain[4], branch_bias[4])
    point_branch = activate(jnp.dot(feature_map, w_point, preferred_element_type=jnp.float32), branch_gain[0], branch_bias[0])
    outputs = [point_branch]
    for branch_index in range(3):
        dilation = dilation_list[branch_index]
        summed = jnp.zeros((height, width_cells, w_point.shape[1]), jnp.float32)
        for row_tap in range(3):
            source = offset_rows(feature_map, (row_tap - 1) * dilation)
            for column_tap in range(3):
                moved = jnp.roll(source, -(column_tap - 1) * dilation, axis=1)
                summed = summed + jnp.dot(moved, w_atrous[branch_index, row_tap, column_tap], preferred_element_type=jnp.float32)
        outputs.append(activate(summed, branch_gain[1 + branch_index], branch_bias[1 + branch_index]))
    outputs.append(jnp.broadcast_to(pool_branch, point_branch.shape))
    joined = jnp.concatenate(outputs, axis=-1)
    return activate(jnp.dot(joined, w_project, preferred_element_type=jnp.float32), project_gain, project_bias)


def reference(features, w_point, w_atrous, w_pool, branch_gain, branch_bias, w_project, project_gain, project_bias, pixel_order):
    projected = whole_map(features, w_point, w_atrous, w_pool, branch_gain, branch_bias, w_project, project_gain, project_bias)
    band_count = ROWS // ROW_DEV
    half_count = W // W_DEV
    device_count = band_count * half_count
    pixels = ROW_DEV * W_DEV
    per_peer = pixels // device_count
    blocks = projected.reshape(band_count, ROW_DEV, half_count, W_DEV, ASPP)
    blocks = jnp.transpose(blocks, (0, 2, 1, 3, 4)).reshape(device_count, pixels, ASPP)
    slots = pixel_order.reshape(band_count, ROW_DEV, half_count, W_DEV)
    slots = jnp.transpose(slots, (0, 2, 1, 3)).reshape(device_count, pixels).astype(jnp.int32)
    outgoing = jnp.take_along_axis(blocks, slots[..., None], axis=1)
    outgoing = outgoing.reshape(device_count, device_count, per_peer, ASPP)
    owned = jnp.transpose(outgoing, (1, 0, 2, 3))
    return owned.reshape(device_count * pixels, ASPP)
```

```python
import jax
import jax.numpy as jnp
from jax import lax
from jax.sharding import PartitionSpec as P

dilation_list = (12, 24, 36)


def passed_along(array, axis, by):
    length = lax.axis_size(axis)
    pairs = [(i, i + by) for i in range(length) if 0 <= i + by < length]
    return lax.ppermute(array, axis, pairs)


def with_halo(array, sides, width):
    for axis, dim in sides:
        size, length = (lax.axis_size(axis), array.shape[dim])
        up = [(i, (i + 1) % size) for i in range(size)]
        down = [(j, i) for i, j in up]
        last = lax.slice_in_dim(array, length - width, length, axis=dim)
        leading = lax.slice_in_dim(array, 0, width, axis=dim)
        before = lax.ppermute(last, axis, up)
        after = lax.ppermute(leading, axis, down)
        array = jnp.concatenate([before, array, after], axis=dim)
    return array


def activate(values, gain, shift_term):
    return jnp.maximum(values * gain + shift_term, 0.0).astype(jnp.bfloat16)


def tap_row(source, weight_row, dilation, reach, width_local):
    summed = None
    for column_tap in range(3):
        start = reach + (column_tap - 1) * dilation
        piece = source[:, start : start + width_local]
        term = jnp.dot(piece, weight_row[column_tap], preferred_element_type=jnp.float32)
        summed = term if summed is None else summed + term
    return summed


def offset_raw(field, offset):
    row_count = field.shape[0]
    band_step = offset // row_count
    remainder = offset - band_step * row_count
    near_rows = field[remainder:]
    pieces = [passed_along(near_rows, "band", -band_step)]
    far_rows = field[:remainder]
    far_step = band_step + 1
    pieces.append(passed_along(far_rows, "band", -far_step))
    return jnp.concatenate(pieces, axis=0)


def shards(
    features,
    w_point,
    w_atrous,
    w_pool,
    branch_gain,
    branch_bias,
    w_project,
    project_gain,
    project_bias,
    pixel_order,
):
    row_count, width_local, channels = features.shape
    band_count = lax.axis_size("band")
    half_count = lax.axis_size("sample")
    device_count = band_count * half_count
    reach = dilation_list[-1]
    local_totals = jnp.sum(features, axis=(0, 1), dtype=jnp.float32)
    totals = lax.psum(local_totals, ("band", "sample"))
    pooled = totals / (row_count * band_count * width_local * half_count)
    pool_input = pooled.astype(jnp.bfloat16)
    pool_value = jnp.dot(pool_input[None, :], w_pool, preferred_element_type=jnp.float32)[0]
    pool_branch = activate(pool_value, branch_gain[4], branch_bias[4])
    point_branch = activate(
        jnp.dot(features, w_point, preferred_element_type=jnp.float32),
        branch_gain[0],
        branch_bias[0],
    )
    widened = with_halo(features, (("sample", 1),), reach)
    atrous_sums = []
    arrived = {}
    for branch_index in (2, 1, 0):
        dilation = dilation_list[branch_index]
        for row_tap in (0, 2):
            partial = tap_row(
                widened, w_atrous[branch_index, row_tap], dilation, reach, width_local
            ).astype(jnp.bfloat16)
            arrived[branch_index, row_tap] = offset_raw(partial, (row_tap - 1) * dilation)
    for branch_index in range(3):
        dilation = dilation_list[branch_index]
        summed = tap_row(widened, w_atrous[branch_index, 1], dilation, reach, width_local)
        for row_tap in (0, 2):
            summed = summed + arrived[branch_index, row_tap].astype(jnp.float32)
        atrous_sums.append(summed)
    outputs = [point_branch]
    for branch_index in range(3):
        outputs.append(
            activate(
                atrous_sums[branch_index],
                branch_gain[1 + branch_index],
                branch_bias[1 + branch_index],
            )
        )
    outputs.append(jnp.broadcast_to(pool_branch, point_branch.shape))
    joined = jnp.concatenate(outputs, axis=-1)
    pixels = row_count * width_local
    per_peer = pixels // device_count
    slots = pixel_order.reshape(pixels)
    projected = activate(
        jnp.dot(joined, w_project, preferred_element_type=jnp.float32), project_gain, project_bias
    )
    outgoing = jnp.take(projected.reshape(pixels, projected.shape[-1]), slots, axis=0)
    outgoing = outgoing.reshape(device_count, per_peer, projected.shape[-1])
    owned = lax.all_to_all(outgoing, ("band", "sample"), split_axis=0, concat_axis=0, tiled=True)
    return owned.reshape(device_count * per_peer, owned.shape[-1])


def solution(mesh):
    in_specs = (
        P("band", "sample", None),
        P(),
        P(),
        P(),
        P(),
        P(),
        P(),
        P(),
        P(),
        P("band", "sample"),
    )
    out_specs = P(("band", "sample"), None)
    return jax.shard_map(shards, mesh=mesh, in_specs=in_specs, out_specs=out_specs, check_vma=False)
```

```python
import functools

import jax
import jax.numpy as jnp
from jax import lax
from jax.experimental import pallas as pl
from jax.experimental.pallas import tpu as pltpu
from jax.sharding import PartitionSpec as P

dilation_list = (12, 24, 36)
pad = 48
vmem_limit = 48 * 2**20
levels = 4


def activate(values, gain, shift_term):
    return jnp.maximum(values * gain + shift_term, 0.0).astype(jnp.bfloat16)


def neighbours_columns(features):
    half_count = lax.axis_size("sample")
    width = features.shape[1]
    leading = features[:, :pad]
    last = features[:, width - pad :]
    up = [(i, (i + 1) % half_count) for i in range(half_count)]
    down = [(j, i) for i, j in up]
    if half_count == 2:
        both = lax.ppermute(jnp.concatenate([leading, last], axis=1), "sample", up)
        return both[:, pad:], both[:, :pad]
    return lax.ppermute(last, "sample", up), lax.ppermute(leading, "sample", down)


def passed_along(array, by):
    band_count = lax.axis_size("band")
    half_count = lax.axis_size("sample")
    level = max(band_count // levels, 1)
    first, second = [], []
    for band in range(band_count):
        goal = band + by
        if not 0 <= goal < band_count:
            continue
        along = goal // level * level + band % level
        within = band // level * level + goal % level
        for half in range(half_count):
            middle = along if half % 2 == 0 or by % level == 0 else within
            first.append((band * half_count + half, middle * half_count + half))
            second.append((middle * half_count + half, goal * half_count + half))
    if not first:
        return jnp.zeros_like(array)
    array = lax.ppermute(array, ("band", "sample"), first)
    if by % level != 0:
        array = lax.ppermute(array, ("band", "sample"), second)
    return array


def total_over_devices(values):
    for axis in ("sample", "band"):
        size = lax.axis_size(axis)
        if size & (size - 1):
            values = lax.psum(values, axis)
            continue
        step = 1
        while step < size:
            values = values + lax.ppermute(values, axis, [(i, i ^ step) for i in range(size)])
            step *= 2
    return values


def split_of(offset, row_count):
    band_step = offset // row_count
    return band_step, offset - band_step * row_count


def taps_body(plan, row_count, x_ref, before_ref, after_ref, *refs):
    weights = refs[: len(plan)]
    outs = refs[len(plan) : -1]
    wide = refs[-1]
    width = x_ref.shape[1]
    row = pl.program_id(0)
    wide[0:pad] = before_ref[0]
    wide[pad : pad + width] = x_ref[0]
    wide[pad + width :] = after_ref[0]
    place = 0
    for (branch, row_tap), w_ref in zip(plan, weights):
        dilation = dilation_list[branch]
        summed = None
        for column_tap in range(3):
            start = pad + (column_tap - 1) * dilation
            term = jnp.dot(
                wide[start : start + width],
                w_ref[0, 0, column_tap],
                preferred_element_type=jnp.float32,
            )
            summed = term if summed is None else summed + term
        summed = summed.astype(jnp.bfloat16)
        _, remainder = split_of((row_tap - 1) * dilation, row_count)
        near = outs[place]
        place += 1
        if remainder:
            far = outs[place]
            place += 1

            @pl.when(row >= remainder)
            def _():
                near[0] = summed

            @pl.when(row < remainder)
            def _():
                far[0] = summed
        else:
            near[0] = summed


def row_taps(features, before, after, w_atrous, plan):
    row_count, width, channels = features.shape
    depth = w_atrous.shape[-1]
    in_specs = [
        pl.BlockSpec((1, width, channels), lambda r: (r, 0, 0)),
        pl.BlockSpec((1, pad, channels), lambda r: (r, 0, 0)),
        pl.BlockSpec((1, pad, channels), lambda r: (r, 0, 0)),
    ]
    out_specs, out_shapes = [], []
    for branch, row_tap in plan:
        in_specs.append(
            pl.BlockSpec(
                (1, 1, 3, channels, depth),
                functools.partial(lambda branch, row_tap, r: (branch, row_tap, 0, 0, 0), branch, row_tap),
            )
        )
        _, remainder = split_of((row_tap - 1) * dilation_list[branch], row_count)
        out_specs.append(
            pl.BlockSpec(
                (1, width, depth),
                functools.partial(lambda remainder, r: (jnp.maximum(r - remainder, 0), 0, 0), remainder),
            )
        )
        out_shapes.append(jax.ShapeDtypeStruct((row_count - remainder, width, depth), jnp.bfloat16))
        if remainder:
            out_specs.append(
                pl.BlockSpec(
                    (1, width, depth),
                    functools.partial(lambda remainder, r: (jnp.minimum(r, remainder - 1), 0, 0), remainder),
                )
            )
            out_shapes.append(jax.ShapeDtypeStruct((remainder, width, depth), jnp.bfloat16))
    return pl.pallas_call(
        functools.partial(taps_body, plan, row_count),
        grid=(row_count,),
        in_specs=in_specs,
        out_specs=out_specs,
        out_shape=out_shapes,
        scratch_shapes=[pltpu.VMEM((width + 2 * pad, channels), jnp.bfloat16)],
        compiler_params=pltpu.CompilerParams(vmem_limit_bytes=vmem_limit),
        cost_estimate=pl.CostEstimate(
            flops=len(plan) * 6 * row_count * width * channels * depth,
            bytes_accessed=2 * (row_count * width * channels + len(plan) * 3 * channels * depth),
            transcendentals=0,
        ),
    )(features, before, after, *([w_atrous] * len(plan)))


def own_body(x_ref, before_ref, after_ref, *refs):
    w_atrous = refs[:3]
    w_point, w_project, gain, shift_term, centre_ref, base_ref, wide = refs[3:]
    width = x_ref.shape[1]
    wide[0:pad] = before_ref[0]
    wide[pad : pad + width] = x_ref[0]
    wide[pad + width :] = after_ref[0]
    for branch, dilation in enumerate(dilation_list):
        summed = None
        for column_tap in range(3):
            start = pad + (column_tap - 1) * dilation
            term = jnp.dot(
                wide[start : start + width],
                w_atrous[branch][0, 0, column_tap],
                preferred_element_type=jnp.float32,
            )
            summed = term if summed is None else summed + term
        centre_ref[branch, 0] = summed
    point = jnp.dot(x_ref[0], w_point[...], preferred_element_type=jnp.float32)
    point = activate(point, gain[0:1], shift_term[0:1])
    base_ref[0] = jnp.dot(point, w_project[...], preferred_element_type=jnp.float32)


def own_rows(features, before, after, w_atrous, w_point, w_project, gain, shift_term):
    row_count, width, channels = features.shape
    depth = w_atrous.shape[-1]
    whole = lambda array: pl.BlockSpec(array.shape, lambda r: (0,) * array.ndim)
    return pl.pallas_call(
        own_body,
        grid=(row_count,),
        in_specs=[
            pl.BlockSpec((1, width, channels), lambda r: (r, 0, 0)),
            pl.BlockSpec((1, pad, channels), lambda r: (r, 0, 0)),
            pl.BlockSpec((1, pad, channels), lambda r: (r, 0, 0)),
        ]
        + [
            pl.BlockSpec(
                (1, 1, 3, channels, depth),
                functools.partial(lambda branch, r: (branch, 1, 0, 0, 0), branch),
            )
            for branch in range(3)
        ]
        + [
            whole(w_point),
            pl.BlockSpec((depth, depth), lambda r: (0, 0)),
            whole(gain),
            whole(shift_term),
        ],
        out_specs=[
            pl.BlockSpec((3, 1, width, depth), lambda r: (0, r, 0, 0)),
            pl.BlockSpec((1, width, depth), lambda r: (r, 0, 0)),
        ],
        out_shape=[
            jax.ShapeDtypeStruct((3, row_count, width, depth), jnp.float32),
            jax.ShapeDtypeStruct((row_count, width, depth), jnp.float32),
        ],
        scratch_shapes=[pltpu.VMEM((width + 2 * pad, channels), jnp.bfloat16)],
        compiler_params=pltpu.CompilerParams(vmem_limit_bytes=vmem_limit),
        cost_estimate=pl.CostEstimate(
            flops=20 * row_count * width * channels * depth,
            bytes_accessed=2 * (row_count * width * channels + 10 * channels * depth)
            + 16 * row_count * width * depth,
            transcendentals=0,
        ),
    )(features, before, after, *([w_atrous] * 3), w_point, w_project, gain, shift_term)


def join_body(plan, remainders, last, base_ref, w_project, gain, shift_term, *refs):
    row = pl.program_id(0)
    total = base_ref[0]
    place = 0
    for branch in plan:
        summed = refs[place][0, 0]
        place += 1
        for row_tap in (0, 2):
            remainder = remainders[branch, row_tap]
            near = refs[place][0].astype(jnp.float32)
            place += 1
            if remainder:
                far = refs[place][0].astype(jnp.float32)
                place += 1
                own_near = base_ref.shape[0] * pl.num_programs(0) - remainder
                near = jnp.where(row < own_near, near, far)
            summed = summed + near
        value = activate(summed, gain[branch + 1 : branch + 2], shift_term[branch + 1 : branch + 2])
        depth = value.shape[-1]
        total = total + jnp.dot(
            value,
            w_project[(branch + 1) * depth : (branch + 2) * depth],
            preferred_element_type=jnp.float32,
        )
    if last:
        pooled, project_gain, project_bias, out = refs[place:]
        out[0] = activate(total + pooled[...], project_gain[...], project_bias[...])
    else:
        refs[place][0] = total


def join(plan, base, centre, arrived, w_project, gain, shift_term, tail=None):
    row_count, width, depth = base.shape
    whole = lambda array: pl.BlockSpec(array.shape, lambda r: (0,) * array.ndim)
    block = pl.BlockSpec((1, width, depth), lambda r: (r, 0, 0))
    operands = [base, w_project, gain, shift_term]
    in_specs = [block, whole(w_project), whole(gain), whole(shift_term)]
    remainders = {}
    for branch in plan:
        operands.append(centre)
        in_specs.append(
            pl.BlockSpec(
                (1, 1, width, depth),
                functools.partial(lambda branch, r: (branch, r, 0, 0), branch),
            )
        )
        for row_tap in (0, 2):
            _, remainder = split_of((row_tap - 1) * dilation_list[branch], row_count)
            remainders[branch, row_tap] = remainder
            near_count = row_count - remainder
            near, far = arrived[branch, row_tap]
            operands.append(near)
            in_specs.append(
                pl.BlockSpec(
                    (1, width, depth),
                    functools.partial(lambda n, r: (jnp.minimum(r, n - 1), 0, 0), near_count),
                )
            )
            if remainder:
                operands.append(far)
                in_specs.append(
                    pl.BlockSpec(
                        (1, width, depth),
                        functools.partial(lambda n, r: (jnp.maximum(r - n, 0), 0, 0), near_count),
                    )
                )
    out_type = jnp.float32
    if tail is not None:
        operands += list(tail)
        in_specs += [whole(array) for array in tail]
        out_type = jnp.bfloat16
    return pl.pallas_call(
        functools.partial(join_body, plan, remainders, tail is not None),
        grid=(row_count,),
        in_specs=in_specs,
        out_specs=block,
        out_shape=jax.ShapeDtypeStruct((row_count, width, depth), out_type),
        compiler_params=pltpu.CompilerParams(vmem_limit_bytes=vmem_limit),
        cost_estimate=pl.CostEstimate(
            flops=len(plan) * 2 * row_count * width * depth * depth,
            bytes_accessed=row_count * width * depth * (8 + 8 * len(plan)),
            transcendentals=0,
        ),
    )(*operands)


def shards(
    features,
    w_point,
    w_atrous,
    w_pool,
    branch_gain,
    branch_bias,
    w_project,
    project_gain,
    project_bias,
    pixel_order,
):
    row_count, width_local, channels = features.shape
    band_count = lax.axis_size("band")
    half_count = lax.axis_size("sample")
    device_count = band_count * half_count
    before, after = neighbours_columns(features)

    arrived = {}
    for calls in (((2, 0),), ((2, 2),), ((1, 0), (1, 2)), ((0, 0), (0, 2))):
        pieces = list(row_taps(features, before, after, w_atrous, calls))
        for branch, row_tap in calls:
            band_step, remainder = split_of((row_tap - 1) * dilation_list[branch], row_count)
            near = passed_along(pieces.pop(0), -band_step)
            far = passed_along(pieces.pop(0), -band_step - 1) if remainder else None
            arrived[branch, row_tap] = (near, far)

    local_totals = jnp.sum(features, axis=(0, 1), dtype=jnp.float32)
    totals = total_over_devices(local_totals)
    pooled = totals / (row_count * band_count * width_local * half_count)
    pool_input = pooled.astype(jnp.bfloat16)
    pool_value = jnp.dot(pool_input[None, :], w_pool, preferred_element_type=jnp.float32)
    pool_branch = activate(pool_value, branch_gain[4:5], branch_bias[4:5])
    depth = w_project.shape[-1]
    pool_projected = jnp.dot(pool_branch, w_project[4 * depth :], preferred_element_type=jnp.float32)

    centre, base = own_rows(
        features, before, after, w_atrous, w_point, w_project, branch_gain, branch_bias
    )
    base = join((2, 1), base, centre, arrived, w_project, branch_gain, branch_bias)
    tail = (pool_projected, project_gain[None, :], project_bias[None, :])
    projected = join((0,), base, centre, arrived, w_project, branch_gain, branch_bias, tail)

    pixels = row_count * width_local
    per_peer = pixels // device_count
    slots = pixel_order.reshape(pixels)
    outgoing = jnp.take(projected.reshape(pixels, depth), slots, axis=0)
    outgoing = outgoing.reshape(device_count, per_peer, depth)
    owned = lax.all_to_all(outgoing, ("band", "sample"), split_axis=0, concat_axis=0, tiled=True)
    return owned.reshape(device_count * per_peer, depth)


def solution(mesh):
    in_specs = (
        P("band", "sample", None),
        P(),
        P(),
        P(),
        P(),
        P(),
        P(),
        P(),
        P(),
        P("band", "sample"),
    )
    out_specs = P(("band", "sample"), None)
    return jax.shard_map(shards, mesh=mesh, in_specs=in_specs, out_specs=out_specs, check_vma=False)
```

```python
import functools

import jax
import jax.numpy as jnp
from jax import lax
from jax.experimental import pallas as pl
from jax.experimental.pallas import tpu as pltpu
from jax.sharding import PartitionSpec as P

dilation_list = (12, 24, 36)
pad = 48
vmem_limit = 48 * 2**20
small_cost = pl.CostEstimate(flops=1024, bytes_accessed=1024, transcendentals=0)
levels = 4


def activate(values, gain, shift_term):
    return jnp.maximum(values * gain + shift_term, 0.0).astype(jnp.bfloat16)


def neighbours_columns(features):
    half_count = lax.axis_size("sample")
    width = features.shape[1]
    leading = features[:, :pad]
    last = features[:, width - pad :]
    up = [(i, (i + 1) % half_count) for i in range(half_count)]
    down = [(j, i) for i, j in up]
    if half_count == 2:
        both = lax.ppermute(jnp.concatenate([leading, last], axis=1), "sample", up)
        return both[:, pad:], both[:, :pad]
    return lax.ppermute(last, "sample", up), lax.ppermute(leading, "sample", down)


def passed_along(array, by):
    band_count = lax.axis_size("band")
    half_count = lax.axis_size("sample")
    level = max(band_count // levels, 1)
    first, second = [], []
    for band in range(band_count):
        goal = band + by
        if not 0 <= goal < band_count:
            continue
        along = goal // level * level + band % level
        within = band // level * level + goal % level
        for half in range(half_count):
            middle = along if half % 2 == 0 or by % level == 0 else within
            first.append((band * half_count + half, middle * half_count + half))
            second.append((middle * half_count + half, goal * half_count + half))
    if not first:
        return jnp.zeros_like(array)
    array = lax.ppermute(array, ("band", "sample"), first)
    if by % level != 0:
        array = lax.ppermute(array, ("band", "sample"), second)
    return array


def total_over_devices(values):
    for axis in ("sample", "band"):
        size = lax.axis_size(axis)
        if size & (size - 1):
            values = lax.psum(values, axis)
            continue
        step = 1
        while step < size:
            values = values + lax.ppermute(values, axis, [(i, i ^ step) for i in range(size)])
            step *= 2
    return values


def split_of(offset, row_count):
    band_step = offset // row_count
    return band_step, offset - band_step * row_count


def taps_body(plan, row_count, x_ref, before_ref, after_ref, *refs):
    weights = refs[: len(plan)]
    outs = refs[len(plan) : -1]
    wide = refs[-1]
    width = x_ref.shape[1]
    row = pl.program_id(0)
    wide[0:pad] = before_ref[0]
    wide[pad : pad + width] = x_ref[0]
    wide[pad + width :] = after_ref[0]
    place = 0
    for (branch, row_tap), w_ref in zip(plan, weights):
        dilation = dilation_list[branch]
        summed = None
        for column_tap in range(3):
            start = pad + (column_tap - 1) * dilation
            term = jnp.dot(
                wide[start : start + width],
                w_ref[0, 0, column_tap],
                preferred_element_type=jnp.float32,
            )
            summed = term if summed is None else summed + term
        summed = summed.astype(jnp.bfloat16)
        _, remainder = split_of((row_tap - 1) * dilation, row_count)
        near = outs[place]
        place += 1
        if remainder:
            far = outs[place]
            place += 1

            @pl.when(row >= remainder)
            def _():
                near[0] = summed

            @pl.when(row < remainder)
            def _():
                far[0] = summed
        else:
            near[0] = summed


def row_taps(features, before, after, w_atrous, plan):
    row_count, width, channels = features.shape
    depth = w_atrous.shape[-1]
    in_specs = [
        pl.BlockSpec((1, width, channels), lambda r: (r, 0, 0)),
        pl.BlockSpec((1, pad, channels), lambda r: (r, 0, 0)),
        pl.BlockSpec((1, pad, channels), lambda r: (r, 0, 0)),
    ]
    out_specs, out_shapes = [], []
    for branch, row_tap in plan:
        in_specs.append(
            pl.BlockSpec(
                (1, 1, 3, channels, depth),
                functools.partial(lambda branch, row_tap, r: (branch, row_tap, 0, 0, 0), branch, row_tap),
            )
        )
        _, remainder = split_of((row_tap - 1) * dilation_list[branch], row_count)
        out_specs.append(
            pl.BlockSpec(
                (1, width, depth),
                functools.partial(lambda remainder, r: (jnp.maximum(r - remainder, 0), 0, 0), remainder),
            )
        )
        out_shapes.append(jax.ShapeDtypeStruct((row_count - remainder, width, depth), jnp.bfloat16))
        if remainder:
            out_specs.append(
                pl.BlockSpec(
                    (1, width, depth),
                    functools.partial(lambda remainder, r: (jnp.minimum(r, remainder - 1), 0, 0), remainder),
                )
            )
            out_shapes.append(jax.ShapeDtypeStruct((remainder, width, depth), jnp.bfloat16))
    return pl.pallas_call(
        functools.partial(taps_body, plan, row_count),
        grid=(row_count,),
        in_specs=in_specs,
        out_specs=out_specs,
        out_shape=out_shapes,
        scratch_shapes=[pltpu.VMEM((width + 2 * pad, channels), jnp.bfloat16)],
        compiler_params=pltpu.CompilerParams(vmem_limit_bytes=vmem_limit),
        cost_estimate=small_cost,
    )(features, before, after, *([w_atrous] * len(plan)))


def own_body(x_ref, before_ref, after_ref, *refs):
    w_atrous = refs[:3]
    w_point, w_project, gain, shift_term, centre_ref, base_ref, wide = refs[3:]
    width = x_ref.shape[1]
    wide[0:pad] = before_ref[0]
    wide[pad : pad + width] = x_ref[0]
    wide[pad + width :] = after_ref[0]
    for branch, dilation in enumerate(dilation_list):
        summed = None
        for column_tap in range(3):
            start = pad + (column_tap - 1) * dilation
            term = jnp.dot(
                wide[start : start + width],
                w_atrous[branch][0, 0, column_tap],
                preferred_element_type=jnp.float32,
            )
            summed = term if summed is None else summed + term
        centre_ref[branch, 0] = summed
    point = jnp.dot(x_ref[0], w_point[...], preferred_element_type=jnp.float32)
    point = activate(point, gain[0:1], shift_term[0:1])
    base_ref[0] = jnp.dot(point, w_project[...], preferred_element_type=jnp.float32)


def own_rows(features, before, after, w_atrous, w_point, w_project, gain, shift_term):
    row_count, width, channels = features.shape
    depth = w_atrous.shape[-1]
    whole = lambda array: pl.BlockSpec(array.shape, lambda r: (0,) * array.ndim)
    return pl.pallas_call(
        own_body,
        grid=(row_count,),
        in_specs=[
            pl.BlockSpec((1, width, channels), lambda r: (r, 0, 0)),
            pl.BlockSpec((1, pad, channels), lambda r: (r, 0, 0)),
            pl.BlockSpec((1, pad, channels), lambda r: (r, 0, 0)),
        ]
        + [
            pl.BlockSpec(
                (1, 1, 3, channels, depth),
                functools.partial(lambda branch, r: (branch, 1, 0, 0, 0), branch),
            )
            for branch in range(3)
        ]
        + [
            whole(w_point),
            pl.BlockSpec((depth, depth), lambda r: (0, 0)),
            whole(gain),
            whole(shift_term),
        ],
        out_specs=[
            pl.BlockSpec((3, 1, width, depth), lambda r: (0, r, 0, 0)),
            pl.BlockSpec((1, width, depth), lambda r: (r, 0, 0)),
        ],
        out_shape=[
            jax.ShapeDtypeStruct((3, row_count, width, depth), jnp.float32),
            jax.ShapeDtypeStruct((row_count, width, depth), jnp.float32),
        ],
        scratch_shapes=[pltpu.VMEM((width + 2 * pad, channels), jnp.bfloat16)],
        compiler_params=pltpu.CompilerParams(vmem_limit_bytes=vmem_limit),
        cost_estimate=small_cost,
    )(features, before, after, *([w_atrous] * 3), w_point, w_project, gain, shift_term)


def join_body(plan, remainders, last, base_ref, w_project, gain, shift_term, *refs):
    row = pl.program_id(0)
    total = base_ref[0]
    place = 0
    for branch in plan:
        summed = refs[place][0, 0]
        place += 1
        for row_tap in (0, 2):
            remainder = remainders[branch, row_tap]
            near = refs[place][0].astype(jnp.float32)
            place += 1
            if remainder:
                far = refs[place][0].astype(jnp.float32)
                place += 1
                own_near = base_ref.shape[0] * pl.num_programs(0) - remainder
                near = jnp.where(row < own_near, near, far)
            summed = summed + near
        value = activate(summed, gain[branch + 1 : branch + 2], shift_term[branch + 1 : branch + 2])
        depth = value.shape[-1]
        total = total + jnp.dot(
            value,
            w_project[(branch + 1) * depth : (branch + 2) * depth],
            preferred_element_type=jnp.float32,
        )
    if last:
        pooled, project_gain, project_bias, out = refs[place:]
        out[0] = activate(total + pooled[...], project_gain[...], project_bias[...])
    else:
        refs[place][0] = total


def join(plan, base, centre, arrived, w_project, gain, shift_term, tail=None):
    row_count, width, depth = base.shape
    whole = lambda array: pl.BlockSpec(array.shape, lambda r: (0,) * array.ndim)
    block = pl.BlockSpec((1, width, depth), lambda r: (r, 0, 0))
    operands = [base, w_project, gain, shift_term]
    in_specs = [block, whole(w_project), whole(gain), whole(shift_term)]
    remainders = {}
    for branch in plan:
        operands.append(centre)
        in_specs.append(
            pl.BlockSpec(
                (1, 1, width, depth),
                functools.partial(lambda branch, r: (branch, r, 0, 0), branch),
            )
        )
        for row_tap in (0, 2):
            _, remainder = split_of((row_tap - 1) * dilation_list[branch], row_count)
            remainders[branch, row_tap] = remainder
            near_count = row_count - remainder
            near, far = arrived[branch, row_tap]
            operands.append(near)
            in_specs.append(
                pl.BlockSpec(
                    (1, width, depth),
                    functools.partial(lambda n, r: (jnp.minimum(r, n - 1), 0, 0), near_count),
                )
            )
            if remainder:
                operands.append(far)
                in_specs.append(
                    pl.BlockSpec(
                        (1, width, depth),
                        functools.partial(lambda n, r: (jnp.maximum(r - n, 0), 0, 0), near_count),
                    )
                )
    out_type = jnp.float32
    if tail is not None:
        operands += list(tail)
        in_specs += [whole(array) for array in tail]
        out_type = jnp.bfloat16
    return pl.pallas_call(
        functools.partial(join_body, plan, remainders, tail is not None),
        grid=(row_count,),
        in_specs=in_specs,
        out_specs=block,
        out_shape=jax.ShapeDtypeStruct((row_count, width, depth), out_type),
        compiler_params=pltpu.CompilerParams(vmem_limit_bytes=vmem_limit),
        cost_estimate=small_cost,
    )(*operands)


def shards(
    features,
    w_point,
    w_atrous,
    w_pool,
    branch_gain,
    branch_bias,
    w_project,
    project_gain,
    project_bias,
    pixel_order,
):
    row_count, width_local, channels = features.shape
    band_count = lax.axis_size("band")
    half_count = lax.axis_size("sample")
    device_count = band_count * half_count
    before, after = neighbours_columns(features)

    arrived = {}
    for calls in (((2, 0),), ((2, 2),), ((1, 0),), ((1, 2),), ((0, 0),), ((0, 2),)):
        pieces = list(row_taps(features, before, after, w_atrous, calls))
        for branch, row_tap in calls:
            band_step, remainder = split_of((row_tap - 1) * dilation_list[branch], row_count)
            near = passed_along(pieces.pop(0), -band_step)
            far = passed_along(pieces.pop(0), -band_step - 1) if remainder else None
            arrived[branch, row_tap] = (near, far)

    local_totals = jnp.sum(features, axis=(0, 1), dtype=jnp.float32)
    totals = total_over_devices(local_totals)
    pooled = totals / (row_count * band_count * width_local * half_count)
    pool_input = pooled.astype(jnp.bfloat16)
    pool_value = jnp.dot(pool_input[None, :], w_pool, preferred_element_type=jnp.float32)
    pool_branch = activate(pool_value, branch_gain[4:5], branch_bias[4:5])
    depth = w_project.shape[-1]
    pool_projected = jnp.dot(pool_branch, w_project[4 * depth :], preferred_element_type=jnp.float32)

    centre, base = own_rows(
        features, before, after, w_atrous, w_point, w_project, branch_gain, branch_bias
    )
    base = join((2, 1), base, centre, arrived, w_project, branch_gain, branch_bias)
    tail = (pool_projected, project_gain[None, :], project_bias[None, :])
    projected = join((0,), base, centre, arrived, w_project, branch_gain, branch_bias, tail)

    pixels = row_count * width_local
    per_peer = pixels // device_count
    slots = pixel_order.reshape(pixels)
    outgoing = jnp.take(projected.reshape(pixels, depth), slots, axis=0)
    outgoing = outgoing.reshape(device_count, per_peer, depth)
    owned = lax.all_to_all(outgoing, ("band", "sample"), split_axis=0, concat_axis=0, tiled=True)
    return owned.reshape(device_count * per_peer, depth)


def solution(mesh):
    in_specs = (
        P("band", "sample", None),
        P(),
        P(),
        P(),
        P(),
        P(),
        P(),
        P(),
        P(),
        P("band", "sample"),
    )
    out_specs = P(("band", "sample"), None)
    return jax.shard_map(shards, mesh=mesh, in_specs=in_specs, out_specs=out_specs, check_vma=False)
```

```python
import functools

import jax
import jax.numpy as jnp
from jax import lax
from jax.experimental import pallas as pl
from jax.experimental.pallas import tpu as pltpu
from jax.sharding import PartitionSpec as P

dilation_list = (12, 24, 36)
pad = 48
vmem_limit = 24 * 2**20
wide_limit = 56 * 2**20
small_cost = pl.CostEstimate(flops=1024, bytes_accessed=1024, transcendentals=0)
routes = {5: "within", 2: "split"}
levels = 4


def activate(values, gain, shift_term):
    return jnp.maximum(values * gain + shift_term, 0.0).astype(jnp.bfloat16)


def neighbours_columns(features):
    half_count = lax.axis_size("sample")
    width = features.shape[1]
    leading = features[:, :pad]
    last = features[:, width - pad :]
    up = [(i, (i + 1) % half_count) for i in range(half_count)]
    down = [(j, i) for i, j in up]
    if half_count == 2:
        both = lax.ppermute(jnp.concatenate([leading, last], axis=1), "sample", up)
        return both[:, pad:], both[:, :pad]
    return lax.ppermute(last, "sample", up), lax.ppermute(leading, "sample", down)


def passed_along(array, by):
    band_count = lax.axis_size("band")
    half_count = lax.axis_size("sample")
    level = max(band_count // levels, 1)
    route = routes.get(abs(by), "direct")
    if by % level == 0:
        route = "direct"
    first, second = [], []
    for band in range(band_count):
        goal = band + by
        if not 0 <= goal < band_count:
            continue
        along = goal // level * level + band % level
        within = band // level * level + goal % level
        for half in range(half_count):
            if route == "direct":
                middle = goal
            elif route == "within" or half % 2:
                middle = within
            else:
                middle = along
            first.append((band * half_count + half, middle * half_count + half))
            second.append((middle * half_count + half, goal * half_count + half))
    if not first:
        return jnp.zeros_like(array), array
    array = lax.ppermute(array, ("band", "sample"), first)
    part_way = array
    if route != "direct":
        array = lax.ppermute(array, ("band", "sample"), second)
    return array, part_way


def total_over_devices(values):
    steps = []
    for axis in ("sample", "band"):
        size = lax.axis_size(axis)
        if size & (size - 1):
            values = lax.psum(values, axis)
            steps.append(values)
            continue
        step = 1
        while step < size:
            values = values + lax.ppermute(values, axis, [(i, i ^ step) for i in range(size)])
            steps.append(values)
            step *= 2
    return values, steps


def split_of(offset, row_count):
    band_step = offset // row_count
    return band_step, offset - band_step * row_count


def taps_body(plan, row_count, token_count, x_ref, before_ref, after_ref, *refs):
    weights = refs[: len(plan)]
    outs = refs[len(plan) + token_count : -1]
    wide = refs[-1]
    width = x_ref.shape[1]
    row = pl.program_id(0)
    wide[0:pad] = before_ref[0]
    wide[pad : pad + width] = x_ref[0]
    wide[pad + width :] = after_ref[0]
    place = 0
    for (branch, row_tap), w_ref in zip(plan, weights):
        dilation = dilation_list[branch]
        summed = None
        for column_tap in range(3):
            start = pad + (column_tap - 1) * dilation
            term = jnp.dot(
                wide[start : start + width],
                w_ref[0, 0, column_tap],
                preferred_element_type=jnp.float32,
            )
            summed = term if summed is None else summed + term
        summed = summed.astype(jnp.bfloat16)
        _, remainder = split_of((row_tap - 1) * dilation, row_count)
        near = outs[place]
        place += 1
        if remainder:
            far = outs[place]
            place += 1

            @pl.when(row >= remainder)
            def _():
                near[0] = summed

            @pl.when(row < remainder)
            def _():
                far[0] = summed
        else:
            near[0] = summed


def row_taps(features, before, after, w_atrous, plan, tokens=()):
    row_count, width, channels = features.shape
    depth = w_atrous.shape[-1]
    in_specs = [
        pl.BlockSpec((1, width, channels), lambda r: (r, 0, 0)),
        pl.BlockSpec((1, pad, channels), lambda r: (r, 0, 0)),
        pl.BlockSpec((1, pad, channels), lambda r: (r, 0, 0)),
    ]
    out_specs, out_shapes = [], []
    for branch, row_tap in plan:
        in_specs.append(
            pl.BlockSpec(
                (1, 1, 3, channels, depth),
                functools.partial(lambda branch, row_tap, r: (branch, row_tap, 0, 0, 0), branch, row_tap),
            )
        )
        _, remainder = split_of((row_tap - 1) * dilation_list[branch], row_count)
        out_specs.append(
            pl.BlockSpec(
                (1, width, depth),
                functools.partial(lambda remainder, r: (jnp.maximum(r - remainder, 0), 0, 0), remainder),
            )
        )
        out_shapes.append(jax.ShapeDtypeStruct((row_count - remainder, width, depth), jnp.bfloat16))
        if remainder:
            out_specs.append(
                pl.BlockSpec(
                    (1, width, depth),
                    functools.partial(lambda remainder, r: (jnp.minimum(r, remainder - 1), 0, 0), remainder),
                )
            )
            out_shapes.append(jax.ShapeDtypeStruct((remainder, width, depth), jnp.bfloat16))
    return pl.pallas_call(
        functools.partial(taps_body, plan, row_count, len(tokens)),
        grid=(row_count,),
        in_specs=in_specs + [pl.BlockSpec(memory_space=pl.ANY)] * len(tokens),
        out_specs=out_specs,
        out_shape=out_shapes,
        scratch_shapes=[pltpu.VMEM((width + 2 * pad, channels), jnp.bfloat16)],
        compiler_params=pltpu.CompilerParams(vmem_limit_bytes=vmem_limit),
        cost_estimate=small_cost,
    )(features, before, after, *([w_atrous] * len(plan)), *tokens)


def own_body(plan, with_point, token_count, x_ref, before_ref, after_ref, *refs):
    weights = refs[: len(plan)]
    place = len(plan)
    if with_point:
        w_point, w_project, gain, shift_term = refs[place : place + 4]
        place += 4
    place += token_count
    centres = refs[place : place + len(plan)]
    extra_ref, wide = refs[place + len(plan) :]
    width = x_ref.shape[1]
    wide[0:pad] = before_ref[0]
    wide[pad : pad + width] = x_ref[0]
    wide[pad + width :] = after_ref[0]
    for branch, w_ref, centre_ref in zip(plan, weights, centres):
        dilation = dilation_list[branch]
        summed = None
        for column_tap in range(3):
            start = pad + (column_tap - 1) * dilation
            term = jnp.dot(
                wide[start : start + width],
                w_ref[0, 0, column_tap],
                preferred_element_type=jnp.float32,
            )
            summed = term if summed is None else summed + term
        centre_ref[0] = summed
    if with_point:
        point = jnp.dot(x_ref[0], w_point[...], preferred_element_type=jnp.float32)
        point = activate(point, gain[0:1], shift_term[0:1])
        extra_ref[0] = jnp.dot(point, w_project[...], preferred_element_type=jnp.float32)


def own_rows(features, before, after, w_atrous, plan, point_operands=None, tokens=()):
    row_count, width, channels = features.shape
    depth = w_atrous.shape[-1]
    whole = lambda array: pl.BlockSpec(array.shape, lambda r: (0,) * array.ndim)
    operands = [features, before, after] + [w_atrous] * len(plan)
    in_specs = [
        pl.BlockSpec((1, width, channels), lambda r: (r, 0, 0)),
        pl.BlockSpec((1, pad, channels), lambda r: (r, 0, 0)),
        pl.BlockSpec((1, pad, channels), lambda r: (r, 0, 0)),
    ]
    for branch in plan:
        in_specs.append(
            pl.BlockSpec(
                (1, 1, 3, channels, depth),
                functools.partial(lambda branch, r: (branch, 1, 0, 0, 0), branch),
            )
        )
    row_block = pl.BlockSpec((1, width, depth), lambda r: (r, 0, 0))
    row_type = jax.ShapeDtypeStruct((row_count, width, depth), jnp.float32)
    if point_operands is not None:
        w_point, w_project, gain, shift_term = point_operands
        operands += [w_point, w_project, gain, shift_term]
        in_specs += [
            whole(w_point),
            pl.BlockSpec((depth, depth), lambda r: (0, 0)),
            whole(gain),
            whole(shift_term),
        ]
        extra_spec, extra_type = row_block, row_type
    else:
        extra_spec = pl.BlockSpec((1, channels), lambda r: (0, 0))
        extra_type = jax.ShapeDtypeStruct((1, channels), jnp.float32)
    operands += list(tokens)
    in_specs += [pl.BlockSpec(memory_space=pl.ANY)] * len(tokens)
    return pl.pallas_call(
        functools.partial(own_body, plan, point_operands is not None, len(tokens)),
        grid=(row_count,),
        in_specs=in_specs,
        out_specs=[row_block] * len(plan) + [extra_spec],
        out_shape=[row_type] * len(plan) + [extra_type],
        scratch_shapes=[pltpu.VMEM((width + 2 * pad, channels), jnp.bfloat16)],
        compiler_params=pltpu.CompilerParams(vmem_limit_bytes=wide_limit),
        cost_estimate=small_cost,
    )(*operands)


def join_body(plan, remainders, last, base_ref, w_project, gain, shift_term, *refs):
    row = pl.program_id(0)
    total = base_ref[0]
    place = 0
    for branch in plan:
        summed = refs[place][0]
        place += 1
        for row_tap in (0, 2):
            remainder = remainders[branch, row_tap]
            near = refs[place][0].astype(jnp.float32)
            place += 1
            if remainder:
                far = refs[place][0].astype(jnp.float32)
                place += 1
                own_near = base_ref.shape[0] * pl.num_programs(0) - remainder
                near = jnp.where(row < own_near, near, far)
            summed = summed + near
        value = activate(summed, gain[branch + 1 : branch + 2], shift_term[branch + 1 : branch + 2])
        depth = value.shape[-1]
        total = total + jnp.dot(
            value,
            w_project[(branch + 1) * depth : (branch + 2) * depth],
            preferred_element_type=jnp.float32,
        )
    if last:
        pooled, project_gain, project_bias, out = refs[place:]
        out[0] = activate(total + pooled[...], project_gain[...], project_bias[...])
    else:
        refs[place][0] = total


def join(plan, base, centre, arrived, w_project, gain, shift_term, tail=None):
    row_count, width, depth = base.shape
    whole = lambda array: pl.BlockSpec(array.shape, lambda r: (0,) * array.ndim)
    block = pl.BlockSpec((1, width, depth), lambda r: (r, 0, 0))
    operands = [base, w_project, gain, shift_term]
    in_specs = [block, whole(w_project), whole(gain), whole(shift_term)]
    remainders = {}
    for branch in plan:
        operands.append(centre[branch])
        in_specs.append(block)
        for row_tap in (0, 2):
            _, remainder = split_of((row_tap - 1) * dilation_list[branch], row_count)
            remainders[branch, row_tap] = remainder
            near_count = row_count - remainder
            near, far = arrived[branch, row_tap]
            operands.append(near)
            in_specs.append(
                pl.BlockSpec(
                    (1, width, depth),
                    functools.partial(lambda n, r: (jnp.minimum(r, n - 1), 0, 0), near_count),
                )
            )
            if remainder:
                operands.append(far)
                in_specs.append(
                    pl.BlockSpec(
                        (1, width, depth),
                        functools.partial(lambda n, r: (jnp.maximum(r - n, 0), 0, 0), near_count),
                    )
                )
    out_type = jnp.float32
    if tail is not None:
        operands += list(tail)
        in_specs += [whole(array) for array in tail]
        out_type = jnp.bfloat16
    return pl.pallas_call(
        functools.partial(join_body, plan, remainders, tail is not None),
        grid=(row_count,),
        in_specs=in_specs,
        out_specs=block,
        out_shape=jax.ShapeDtypeStruct((row_count, width, depth), out_type),
        compiler_params=pltpu.CompilerParams(vmem_limit_bytes=wide_limit),
        cost_estimate=small_cost,
    )(*operands)


def shards(
    features,
    w_point,
    w_atrous,
    w_pool,
    branch_gain,
    branch_bias,
    w_project,
    project_gain,
    project_bias,
    pixel_order,
):
    row_count, width_local, channels = features.shape
    band_count = lax.axis_size("band")
    half_count = lax.axis_size("sample")
    device_count = band_count * half_count
    before, after = neighbours_columns(features)

    arrived, part_way = {}, {}

    def send(branch, row_tap, tokens=()):
        near, *far = row_taps(features, before, after, w_atrous, ((branch, row_tap),), tokens)
        band_step, remainder = split_of((row_tap - 1) * dilation_list[branch], row_count)
        near, near_way = passed_along(near, -band_step)
        far, far_way = passed_along(far[0], -band_step - 1) if far else (None, near_way)
        arrived[branch, row_tap] = (near, far)
        ways = (near_way, far_way) if near_way.shape[0] < far_way.shape[0] else (far_way, near_way)
        part_way[branch, row_tap] = ways

    totals, steps = total_over_devices(jnp.sum(features, axis=(0, 1), dtype=jnp.float32))
    order = ((2, 0), (2, 2), (1, 0), (1, 2), (0, 0), (0, 2))
    for place, (branch, row_tap) in enumerate(order):
        send(branch, row_tap, steps[place - 1 : place] if place else ())
    centre = {}
    centre[2], centre[1], centre[0], base = own_rows(
        features,
        before,
        after,
        w_atrous,
        (2, 1, 0),
        (w_point, w_project, branch_gain, branch_bias),
        [part_way[2, 0][1]],
    )
    pooled = totals / (row_count * band_count * width_local * half_count)
    pool_input = pooled.astype(jnp.bfloat16)
    pool_value = jnp.dot(pool_input[None, :], w_pool, preferred_element_type=jnp.float32)
    pool_branch = activate(pool_value, branch_gain[4:5], branch_bias[4:5])
    depth = w_project.shape[-1]
    pool_projected = jnp.dot(pool_branch, w_project[4 * depth :], preferred_element_type=jnp.float32)

    base = join((2, 1), base, centre, arrived, w_project, branch_gain, branch_bias)
    tail = (pool_projected, project_gain[None, :], project_bias[None, :])
    projected = join((0,), base, centre, arrived, w_project, branch_gain, branch_bias, tail)

    pixels = row_count * width_local
    per_peer = pixels // device_count
    slots = pixel_order.reshape(pixels)
    outgoing = jnp.take(projected.reshape(pixels, depth), slots, axis=0)
    outgoing = outgoing.reshape(device_count, per_peer, depth)
    owned = lax.all_to_all(outgoing, ("band", "sample"), split_axis=0, concat_axis=0, tiled=True)
    return owned.reshape(device_count * per_peer, depth)


def solution(mesh):
    in_specs = (
        P("band", "sample", None),
        P(),
        P(),
        P(),
        P(),
        P(),
        P(),
        P(),
        P(),
        P("band", "sample"),
    )
    out_specs = P(("band", "sample"), None)
    return jax.shard_map(shards, mesh=mesh, in_specs=in_specs, out_specs=out_specs, check_vma=False)
```

```python
import functools

import jax
import jax.numpy as jnp
from jax import lax
from jax.experimental import pallas as pl
from jax.experimental.pallas import tpu as pltpu
from jax.sharding import PartitionSpec as P

dilation_list = (12, 24, 36)
pad = 48
vmem_limit = 24 * 2**20
wide_limit = 56 * 2**20
small_cost = pl.CostEstimate(flops=1024, bytes_accessed=1024, transcendentals=0)
routes = {5: "within", 2: "split"}
own_place = 4
levels = 4


def activate(values, gain, shift_term):
    return jnp.maximum(values * gain + shift_term, 0.0).astype(jnp.bfloat16)


def neighbours_columns(features):
    half_count = lax.axis_size("sample")
    width = features.shape[1]
    leading = features[:, :pad]
    last = features[:, width - pad :]
    up = [(i, (i + 1) % half_count) for i in range(half_count)]
    down = [(j, i) for i, j in up]
    if half_count == 2:
        both = lax.ppermute(jnp.concatenate([leading, last], axis=1), "sample", up)
        return both[:, pad:], both[:, :pad]
    return lax.ppermute(last, "sample", up), lax.ppermute(leading, "sample", down)


def passed_along(array, by, hold=None):
    band_count = lax.axis_size("band")
    half_count = lax.axis_size("sample")
    level = max(band_count // levels, 1)
    route = routes.get(abs(by), "direct")
    if by % level == 0:
        route = "direct"
    first, second = [], []
    for band in range(band_count):
        goal = band + by
        if not 0 <= goal < band_count:
            continue
        along = goal // level * level + band % level
        within = band // level * level + goal % level
        for half in range(half_count):
            if route == "direct":
                middle = goal
            elif route == "within" or half % 2:
                middle = within
            else:
                middle = along
            first.append((band * half_count + half, middle * half_count + half))
            second.append((middle * half_count + half, goal * half_count + half))
    if not first:
        return jnp.zeros_like(array), array
    array = lax.ppermute(array, ("band", "sample"), first)
    part_way = array
    if route != "direct":
        if hold is not None:
            array, _ = lax.optimization_barrier((array, hold))
        array = lax.ppermute(array, ("band", "sample"), second)
    return array, part_way


def total_over_devices(values):
    steps = []
    for axis in ("sample", "band"):
        size = lax.axis_size(axis)
        if size & (size - 1):
            values = lax.psum(values, axis)
            steps.append(values)
            continue
        step = 1
        while step < size:
            values = values + lax.ppermute(values, axis, [(i, i ^ step) for i in range(size)])
            steps.append(values)
            step *= 2
    return values, steps


def split_of(offset, row_count):
    band_step = offset // row_count
    return band_step, offset - band_step * row_count


def taps_body(plan, row_count, token_count, x_ref, before_ref, after_ref, *refs):
    weights = refs[: len(plan)]
    outs = refs[len(plan) + token_count : -1]
    wide = refs[-1]
    width = x_ref.shape[1]
    row = pl.program_id(0)
    wide[0:pad] = before_ref[0]
    wide[pad : pad + width] = x_ref[0]
    wide[pad + width :] = after_ref[0]
    place = 0
    for (branch, row_tap), w_ref in zip(plan, weights):
        dilation = dilation_list[branch]
        summed = None
        for column_tap in range(3):
            start = pad + (column_tap - 1) * dilation
            term = jnp.dot(
                wide[start : start + width],
                w_ref[0, 0, column_tap],
                preferred_element_type=jnp.float32,
            )
            summed = term if summed is None else summed + term
        summed = summed.astype(jnp.bfloat16)
        _, remainder = split_of((row_tap - 1) * dilation, row_count)
        near = outs[place]
        place += 1
        if remainder:
            far = outs[place]
            place += 1

            @pl.when(row >= remainder)
            def _():
                near[0] = summed

            @pl.when(row < remainder)
            def _():
                far[0] = summed
        else:
            near[0] = summed


def row_taps(features, before, after, w_atrous, plan, tokens=()):
    row_count, width, channels = features.shape
    depth = w_atrous.shape[-1]
    in_specs = [
        pl.BlockSpec((1, width, channels), lambda r: (r, 0, 0)),
        pl.BlockSpec((1, pad, channels), lambda r: (r, 0, 0)),
        pl.BlockSpec((1, pad, channels), lambda r: (r, 0, 0)),
    ]
    out_specs, out_shapes = [], []
    for branch, row_tap in plan:
        in_specs.append(
            pl.BlockSpec(
                (1, 1, 3, channels, depth),
                functools.partial(lambda branch, row_tap, r: (branch, row_tap, 0, 0, 0), branch, row_tap),
            )
        )
        _, remainder = split_of((row_tap - 1) * dilation_list[branch], row_count)
        out_specs.append(
            pl.BlockSpec(
                (1, width, depth),
                functools.partial(lambda remainder, r: (jnp.maximum(r - remainder, 0), 0, 0), remainder),
            )
        )
        out_shapes.append(jax.ShapeDtypeStruct((row_count - remainder, width, depth), jnp.bfloat16))
        if remainder:
            out_specs.append(
                pl.BlockSpec(
                    (1, width, depth),
                    functools.partial(lambda remainder, r: (jnp.minimum(r, remainder - 1), 0, 0), remainder),
                )
            )
            out_shapes.append(jax.ShapeDtypeStruct((remainder, width, depth), jnp.bfloat16))
    return pl.pallas_call(
        functools.partial(taps_body, plan, row_count, len(tokens)),
        grid=(row_count,),
        in_specs=in_specs + [pl.BlockSpec(memory_space=pl.ANY)] * len(tokens),
        out_specs=out_specs,
        out_shape=out_shapes,
        scratch_shapes=[pltpu.VMEM((width + 2 * pad, channels), jnp.bfloat16)],
        compiler_params=pltpu.CompilerParams(vmem_limit_bytes=vmem_limit),
        cost_estimate=small_cost,
    )(features, before, after, *([w_atrous] * len(plan)), *tokens)


def own_body(plan, with_point, token_count, x_ref, before_ref, after_ref, *refs):
    weights = refs[: len(plan)]
    place = len(plan)
    if with_point:
        w_point, w_project, gain, shift_term = refs[place : place + 4]
        place += 4
    place += token_count
    centres = refs[place : place + len(plan)]
    extra_ref, wide = refs[place + len(plan) :]
    width = x_ref.shape[1]
    wide[0:pad] = before_ref[0]
    wide[pad : pad + width] = x_ref[0]
    wide[pad + width :] = after_ref[0]
    for branch, w_ref, centre_ref in zip(plan, weights, centres):
        dilation = dilation_list[branch]
        summed = None
        for column_tap in range(3):
            start = pad + (column_tap - 1) * dilation
            term = jnp.dot(
                wide[start : start + width],
                w_ref[0, 0, column_tap],
                preferred_element_type=jnp.float32,
            )
            summed = term if summed is None else summed + term
        centre_ref[0] = summed
    if with_point:
        point = jnp.dot(x_ref[0], w_point[...], preferred_element_type=jnp.float32)
        point = activate(point, gain[0:1], shift_term[0:1])
        extra_ref[0] = jnp.dot(point, w_project[...], preferred_element_type=jnp.float32)


def own_rows(features, before, after, w_atrous, plan, point_operands=None, tokens=()):
    row_count, width, channels = features.shape
    depth = w_atrous.shape[-1]
    whole = lambda array: pl.BlockSpec(array.shape, lambda r: (0,) * array.ndim)
    operands = [features, before, after] + [w_atrous] * len(plan)
    in_specs = [
        pl.BlockSpec((1, width, channels), lambda r: (r, 0, 0)),
        pl.BlockSpec((1, pad, channels), lambda r: (r, 0, 0)),
        pl.BlockSpec((1, pad, channels), lambda r: (r, 0, 0)),
    ]
    for branch in plan:
        in_specs.append(
            pl.BlockSpec(
                (1, 1, 3, channels, depth),
                functools.partial(lambda branch, r: (branch, 1, 0, 0, 0), branch),
            )
        )
    row_block = pl.BlockSpec((1, width, depth), lambda r: (r, 0, 0))
    row_type = jax.ShapeDtypeStruct((row_count, width, depth), jnp.float32)
    if point_operands is not None:
        w_point, w_project, gain, shift_term = point_operands
        operands += [w_point, w_project, gain, shift_term]
        in_specs += [
            whole(w_point),
            pl.BlockSpec((depth, depth), lambda r: (0, 0)),
            whole(gain),
            whole(shift_term),
        ]
        extra_spec, extra_type = row_block, row_type
    else:
        extra_spec = pl.BlockSpec((1, channels), lambda r: (0, 0))
        extra_type = jax.ShapeDtypeStruct((1, channels), jnp.float32)
    operands += list(tokens)
    in_specs += [pl.BlockSpec(memory_space=pl.ANY)] * len(tokens)
    return pl.pallas_call(
        functools.partial(own_body, plan, point_operands is not None, len(tokens)),
        grid=(row_count,),
        in_specs=in_specs,
        out_specs=[row_block] * len(plan) + [extra_spec],
        out_shape=[row_type] * len(plan) + [extra_type],
        scratch_shapes=[pltpu.VMEM((width + 2 * pad, channels), jnp.bfloat16)],
        compiler_params=pltpu.CompilerParams(vmem_limit_bytes=wide_limit),
        cost_estimate=small_cost,
    )(*operands)


def join_body(plan, remainders, last, base_ref, w_project, gain, shift_term, *refs):
    row = pl.program_id(0)
    total = base_ref[0]
    place = 0
    for branch in plan:
        summed = refs[place][0]
        place += 1
        for row_tap in (0, 2):
            remainder = remainders[branch, row_tap]
            near = refs[place][0].astype(jnp.float32)
            place += 1
            if remainder:
                far = refs[place][0].astype(jnp.float32)
                place += 1
                own_near = base_ref.shape[0] * pl.num_programs(0) - remainder
                near = jnp.where(row < own_near, near, far)
            summed = summed + near
        value = activate(summed, gain[branch + 1 : branch + 2], shift_term[branch + 1 : branch + 2])
        depth = value.shape[-1]
        total = total + jnp.dot(
            value,
            w_project[(branch + 1) * depth : (branch + 2) * depth],
            preferred_element_type=jnp.float32,
        )
    if last:
        pooled, project_gain, project_bias, out = refs[place:]
        out[0] = activate(total + pooled[...], project_gain[...], project_bias[...])
    else:
        refs[place][0] = total


def join(plan, base, centre, arrived, w_project, gain, shift_term, tail=None):
    row_count, width, depth = base.shape
    whole = lambda array: pl.BlockSpec(array.shape, lambda r: (0,) * array.ndim)
    block = pl.BlockSpec((1, width, depth), lambda r: (r, 0, 0))
    operands = [base, w_project, gain, shift_term]
    in_specs = [block, whole(w_project), whole(gain), whole(shift_term)]
    remainders = {}
    for branch in plan:
        operands.append(centre[branch])
        in_specs.append(block)
        for row_tap in (0, 2):
            _, remainder = split_of((row_tap - 1) * dilation_list[branch], row_count)
            remainders[branch, row_tap] = remainder
            near_count = row_count - remainder
            near, far = arrived[branch, row_tap]
            operands.append(near)
            in_specs.append(
                pl.BlockSpec(
                    (1, width, depth),
                    functools.partial(lambda n, r: (jnp.minimum(r, n - 1), 0, 0), near_count),
                )
            )
            if remainder:
                operands.append(far)
                in_specs.append(
                    pl.BlockSpec(
                        (1, width, depth),
                        functools.partial(lambda n, r: (jnp.maximum(r - n, 0), 0, 0), near_count),
                    )
                )
    out_type = jnp.float32
    if tail is not None:
        operands += list(tail)
        in_specs += [whole(array) for array in tail]
        out_type = jnp.bfloat16
    return pl.pallas_call(
        functools.partial(join_body, plan, remainders, tail is not None),
        grid=(row_count,),
        in_specs=in_specs,
        out_specs=block,
        out_shape=jax.ShapeDtypeStruct((row_count, width, depth), out_type),
        compiler_params=pltpu.CompilerParams(vmem_limit_bytes=wide_limit),
        cost_estimate=small_cost,
    )(*operands)


def shards(
    features,
    w_point,
    w_atrous,
    w_pool,
    branch_gain,
    branch_bias,
    w_project,
    project_gain,
    project_bias,
    pixel_order,
):
    row_count, width_local, channels = features.shape
    band_count = lax.axis_size("band")
    half_count = lax.axis_size("sample")
    device_count = band_count * half_count
    before, after = neighbours_columns(features)

    arrived, part_way = {}, {}

    def send(branch, row_tap, tokens=(), hold=None):
        near, *far = row_taps(features, before, after, w_atrous, ((branch, row_tap),), tokens)
        band_step, remainder = split_of((row_tap - 1) * dilation_list[branch], row_count)
        near, near_way = passed_along(near, -band_step, hold)
        far, far_way = passed_along(far[0], -band_step - 1, hold) if far else (None, near_way)
        arrived[branch, row_tap] = (near, far)
        ways = (near_way, far_way) if near_way.shape[0] < far_way.shape[0] else (far_way, near_way)
        part_way[branch, row_tap] = ways

    totals, steps = total_over_devices(jnp.sum(features, axis=(0, 1), dtype=jnp.float32))
    order = ((2, 0), (2, 2), (1, 0), (1, 2), (0, 0), (0, 2))
    centre, base = {}, None
    for place, (branch, row_tap) in enumerate(order):
        if place == own_place:
            centre[2], centre[1], centre[0], base = own_rows(
                features,
                before,
                after,
                w_atrous,
                (2, 1, 0),
                (w_point, w_project, branch_gain, branch_bias),
                [part_way[2, 0][1]],
            )
        send(branch, row_tap, steps[place - 1 : place] if place else (), base)

    pooled = totals / (row_count * band_count * width_local * half_count)
    pool_input = pooled.astype(jnp.bfloat16)
    pool_value = jnp.dot(pool_input[None, :], w_pool, preferred_element_type=jnp.float32)
    pool_branch = activate(pool_value, branch_gain[4:5], branch_bias[4:5])
    depth = w_project.shape[-1]
    pool_projected = jnp.dot(pool_branch, w_project[4 * depth :], preferred_element_type=jnp.float32)

    base = join((2, 1), base, centre, arrived, w_project, branch_gain, branch_bias)
    tail = (pool_projected, project_gain[None, :], project_bias[None, :])
    projected = join((0,), base, centre, arrived, w_project, branch_gain, branch_bias, tail)

    pixels = row_count * width_local
    per_peer = pixels // device_count
    slots = pixel_order.reshape(pixels)
    outgoing = jnp.take(projected.reshape(pixels, depth), slots, axis=0)
    outgoing = outgoing.reshape(device_count, per_peer, depth)
    owned = lax.all_to_all(outgoing, ("band", "sample"), split_axis=0, concat_axis=0, tiled=True)
    return owned.reshape(device_count * per_peer, depth)


def solution(mesh):
    in_specs = (
        P("band", "sample", None),
        P(),
        P(),
        P(),
        P(),
        P(),
        P(),
        P(),
        P(),
        P("band", "sample"),
    )
    out_specs = P(("band", "sample"), None)
    return jax.shard_map(shards, mesh=mesh, in_specs=in_specs, out_specs=out_specs, check_vma=False)
```

```python
import functools

import jax
import jax.numpy as jnp
from jax import lax
from jax.experimental import pallas as pl
from jax.experimental.pallas import tpu as pltpu
from jax.sharding import PartitionSpec as P

dilation_list = (12, 24, 36)
pad = 48
vmem_limit = 24 * 2**20
wide_limit = 56 * 2**20
small_cost = pl.CostEstimate(flops=1024, bytes_accessed=1024, transcendentals=0)
routes = {5: "within", 2: "split"}
own_place = 4
levels = 4


def activate(values, gain, shift_term):
    return jnp.maximum(values * gain + shift_term, 0.0).astype(jnp.bfloat16)


def neighbours_columns(features):
    half_count = lax.axis_size("sample")
    width = features.shape[1]
    leading = features[:, :pad]
    last = features[:, width - pad :]
    up = [(i, (i + 1) % half_count) for i in range(half_count)]
    down = [(j, i) for i, j in up]
    if half_count == 2:
        both = lax.ppermute(jnp.concatenate([leading, last], axis=1), "sample", up)
        return both[:, pad:], both[:, :pad]
    return lax.ppermute(last, "sample", up), lax.ppermute(leading, "sample", down)


def passed_along(array, by, hold=None):
    band_count = lax.axis_size("band")
    half_count = lax.axis_size("sample")
    level = max(band_count // levels, 1)
    route = routes.get(abs(by), "direct")
    if by % level == 0:
        route = "direct"
    first, second = [], []
    for band in range(band_count):
        goal = band + by
        if not 0 <= goal < band_count:
            continue
        along = goal // level * level + band % level
        within = band // level * level + goal % level
        for half in range(half_count):
            if route == "direct":
                middle = goal
            elif route == "within" or half % 2:
                middle = within
            else:
                middle = along
            first.append((band * half_count + half, middle * half_count + half))
            second.append((middle * half_count + half, goal * half_count + half))
    if not first:
        return jnp.zeros_like(array), array
    array = lax.ppermute(array, ("band", "sample"), first)
    part_way = array
    if route != "direct":
        if hold is not None:
            array, _ = lax.optimization_barrier((array, hold))
        array = lax.ppermute(array, ("band", "sample"), second)
    return array, part_way


def total_over_devices(values):
    steps = []
    for axis in ("sample", "band"):
        size = lax.axis_size(axis)
        if size & (size - 1):
            values = lax.psum(values, axis)
            steps.append(values)
            continue
        step = 1
        while step < size:
            values = values + lax.ppermute(values, axis, [(i, i ^ step) for i in range(size)])
            steps.append(values)
            step *= 2
    return values, steps


def split_of(offset, row_count):
    band_step = offset // row_count
    return band_step, offset - band_step * row_count


def taps_body(plan, row_count, token_count, x_ref, before_ref, after_ref, *refs):
    weights = refs[: len(plan)]
    outs = refs[len(plan) + token_count : -1]
    wide = refs[-1]
    width = x_ref.shape[1]
    row = pl.program_id(0)
    wide[0:pad] = before_ref[0]
    wide[pad : pad + width] = x_ref[0]
    wide[pad + width :] = after_ref[0]
    place = 0
    for (branch, row_tap), w_ref in zip(plan, weights):
        dilation = dilation_list[branch]
        summed = None
        for column_tap in range(3):
            start = pad + (column_tap - 1) * dilation
            term = jnp.dot(
                wide[start : start + width],
                w_ref[0, 0, column_tap],
                preferred_element_type=jnp.float32,
            )
            summed = term if summed is None else summed + term
        summed = summed.astype(jnp.bfloat16)
        _, remainder = split_of((row_tap - 1) * dilation, row_count)
        near = outs[place]
        place += 1
        if remainder:
            far = outs[place]
            place += 1

            @pl.when(row >= remainder)
            def _():
                near[0] = summed

            @pl.when(row < remainder)
            def _():
                far[0] = summed
        else:
            near[0] = summed


def row_taps(features, before, after, w_atrous, plan, tokens=()):
    row_count, width, channels = features.shape
    depth = w_atrous.shape[-1]
    in_specs = [
        pl.BlockSpec((1, width, channels), lambda r: (r, 0, 0)),
        pl.BlockSpec((1, pad, channels), lambda r: (r, 0, 0)),
        pl.BlockSpec((1, pad, channels), lambda r: (r, 0, 0)),
    ]
    out_specs, out_shapes = [], []
    for branch, row_tap in plan:
        in_specs.append(
            pl.BlockSpec(
                (1, 1, 3, channels, depth),
                functools.partial(lambda branch, row_tap, r: (branch, row_tap, 0, 0, 0), branch, row_tap),
            )
        )
        _, remainder = split_of((row_tap - 1) * dilation_list[branch], row_count)
        out_specs.append(
            pl.BlockSpec(
                (1, width, depth),
                functools.partial(lambda remainder, r: (jnp.maximum(r - remainder, 0), 0, 0), remainder),
            )
        )
        out_shapes.append(jax.ShapeDtypeStruct((row_count - remainder, width, depth), jnp.bfloat16))
        if remainder:
            out_specs.append(
                pl.BlockSpec(
                    (1, width, depth),
                    functools.partial(lambda remainder, r: (jnp.minimum(r, remainder - 1), 0, 0), remainder),
                )
            )
            out_shapes.append(jax.ShapeDtypeStruct((remainder, width, depth), jnp.bfloat16))
    return pl.pallas_call(
        functools.partial(taps_body, plan, row_count, len(tokens)),
        grid=(row_count,),
        in_specs=in_specs + [pl.BlockSpec(memory_space=pl.ANY)] * len(tokens),
        out_specs=out_specs,
        out_shape=out_shapes,
        scratch_shapes=[pltpu.VMEM((width + 2 * pad, channels), jnp.bfloat16)],
        compiler_params=pltpu.CompilerParams(vmem_limit_bytes=vmem_limit),
        cost_estimate=small_cost,
    )(features, before, after, *([w_atrous] * len(plan)), *tokens)


def own_body(plan, with_point, token_count, x_ref, before_ref, after_ref, *refs):
    weights = refs[: len(plan)]
    place = len(plan)
    if with_point:
        w_point, w_project, gain, shift_term = refs[place : place + 4]
        place += 4
    place += token_count
    centres = refs[place : place + len(plan)]
    extra_ref, wide = refs[place + len(plan) :]
    width = x_ref.shape[1]
    wide[0:pad] = before_ref[0]
    wide[pad : pad + width] = x_ref[0]
    wide[pad + width :] = after_ref[0]
    for branch, w_ref, centre_ref in zip(plan, weights, centres):
        dilation = dilation_list[branch]
        summed = None
        for column_tap in range(3):
            start = pad + (column_tap - 1) * dilation
            term = jnp.dot(
                wide[start : start + width],
                w_ref[0, 0, column_tap],
                preferred_element_type=jnp.float32,
            )
            summed = term if summed is None else summed + term
        centre_ref[0] = summed
    if with_point:
        point = jnp.dot(x_ref[0], w_point[...], preferred_element_type=jnp.float32)
        point = activate(point, gain[0:1], shift_term[0:1])
        extra_ref[0] = jnp.dot(point, w_project[...], preferred_element_type=jnp.float32)


def own_rows(features, before, after, w_atrous, plan, point_operands=None, tokens=()):
    row_count, width, channels = features.shape
    depth = w_atrous.shape[-1]
    whole = lambda array: pl.BlockSpec(array.shape, lambda r: (0,) * array.ndim)
    operands = [features, before, after] + [w_atrous] * len(plan)
    in_specs = [
        pl.BlockSpec((1, width, channels), lambda r: (r, 0, 0)),
        pl.BlockSpec((1, pad, channels), lambda r: (r, 0, 0)),
        pl.BlockSpec((1, pad, channels), lambda r: (r, 0, 0)),
    ]
    for branch in plan:
        in_specs.append(
            pl.BlockSpec(
                (1, 1, 3, channels, depth),
                functools.partial(lambda branch, r: (branch, 1, 0, 0, 0), branch),
            )
        )
    row_block = pl.BlockSpec((1, width, depth), lambda r: (r, 0, 0))
    row_type = jax.ShapeDtypeStruct((row_count, width, depth), jnp.float32)
    if point_operands is not None:
        w_point, w_project, gain, shift_term = point_operands
        operands += [w_point, w_project, gain, shift_term]
        in_specs += [
            whole(w_point),
            pl.BlockSpec((depth, depth), lambda r: (0, 0)),
            whole(gain),
            whole(shift_term),
        ]
        extra_spec, extra_type = row_block, row_type
    else:
        extra_spec = pl.BlockSpec((1, channels), lambda r: (0, 0))
        extra_type = jax.ShapeDtypeStruct((1, channels), jnp.float32)
    operands += list(tokens)
    in_specs += [pl.BlockSpec(memory_space=pl.ANY)] * len(tokens)
    return pl.pallas_call(
        functools.partial(own_body, plan, point_operands is not None, len(tokens)),
        grid=(row_count,),
        in_specs=in_specs,
        out_specs=[row_block] * len(plan) + [extra_spec],
        out_shape=[row_type] * len(plan) + [extra_type],
        scratch_shapes=[pltpu.VMEM((width + 2 * pad, channels), jnp.bfloat16)],
        compiler_params=pltpu.CompilerParams(vmem_limit_bytes=wide_limit),
        cost_estimate=small_cost,
    )(*operands)


def join_body(plan, remainders, last, base_ref, w_project, gain, shift_term, *refs):
    row = pl.program_id(0)
    total = base_ref[0]
    place = 0
    for branch in plan:
        summed = refs[place][0]
        place += 1
        for row_tap in (0, 2):
            remainder = remainders[branch, row_tap]
            near = refs[place][0].astype(jnp.float32)
            place += 1
            if remainder:
                far = refs[place][0].astype(jnp.float32)
                place += 1
                own_near = base_ref.shape[0] * pl.num_programs(0) - remainder
                near = jnp.where(row < own_near, near, far)
            summed = summed + near
        value = activate(summed, gain[branch + 1 : branch + 2], shift_term[branch + 1 : branch + 2])
        depth = value.shape[-1]
        total = total + jnp.dot(
            value,
            w_project[(branch + 1) * depth : (branch + 2) * depth],
            preferred_element_type=jnp.float32,
        )
    if last:
        pooled, project_gain, project_bias, slots, out, cells = refs[place:]
        width = total.shape[0]
        pixels = cells.shape[0]
        cells[pl.ds(pl.multiple_of(row * width, width), width)] = activate(
            total + pooled[...], project_gain[...], project_bias[...]
        )

        @pl.when(row == pl.num_programs(0) - 1)
        def _():
            for start in range(0, pixels, width):
                place_of = lax.broadcasted_iota(jnp.int32, (width, pixels), 1)
                picked = jnp.where(slots[start : start + width] == place_of, 1.0, 0.0)
                out[start : start + width] = jnp.dot(
                    picked.astype(jnp.bfloat16), cells[...], preferred_element_type=jnp.float32
                ).astype(jnp.bfloat16)
    else:
        refs[place][0] = total


def join(plan, base, centre, arrived, w_project, gain, shift_term, tail=None):
    row_count, width, depth = base.shape
    whole = lambda array: pl.BlockSpec(array.shape, lambda r: (0,) * array.ndim)
    block = pl.BlockSpec((1, width, depth), lambda r: (r, 0, 0))
    operands = [base, w_project, gain, shift_term]
    in_specs = [block, whole(w_project), whole(gain), whole(shift_term)]
    remainders = {}
    for branch in plan:
        operands.append(centre[branch])
        in_specs.append(block)
        for row_tap in (0, 2):
            _, remainder = split_of((row_tap - 1) * dilation_list[branch], row_count)
            remainders[branch, row_tap] = remainder
            near_count = row_count - remainder
            near, far = arrived[branch, row_tap]
            operands.append(near)
            in_specs.append(
                pl.BlockSpec(
                    (1, width, depth),
                    functools.partial(lambda n, r: (jnp.minimum(r, n - 1), 0, 0), near_count),
                )
            )
            if remainder:
                operands.append(far)
                in_specs.append(
                    pl.BlockSpec(
                        (1, width, depth),
                        functools.partial(lambda n, r: (jnp.maximum(r - n, 0), 0, 0), near_count),
                    )
                )
    out_spec, scratch = block, []
    out_type = jax.ShapeDtypeStruct((row_count, width, depth), jnp.float32)
    if tail is not None:
        operands += list(tail)
        in_specs += [whole(array) for array in tail]
        out_type = jax.ShapeDtypeStruct((row_count * width, depth), jnp.bfloat16)
        out_spec = pl.BlockSpec((row_count * width, depth), lambda r: (0, 0))
        scratch = [pltpu.VMEM((row_count * width, depth), jnp.bfloat16)]
    return pl.pallas_call(
        functools.partial(join_body, plan, remainders, tail is not None),
        grid=(row_count,),
        in_specs=in_specs,
        out_specs=out_spec,
        out_shape=out_type,
        scratch_shapes=scratch,
        compiler_params=pltpu.CompilerParams(vmem_limit_bytes=wide_limit),
        cost_estimate=small_cost,
    )(*operands)


def shards(
    features,
    w_point,
    w_atrous,
    w_pool,
    branch_gain,
    branch_bias,
    w_project,
    project_gain,
    project_bias,
    pixel_order,
):
    row_count, width_local, channels = features.shape
    band_count = lax.axis_size("band")
    half_count = lax.axis_size("sample")
    device_count = band_count * half_count
    before, after = neighbours_columns(features)

    arrived, part_way = {}, {}

    def send(branch, row_tap, tokens=(), hold=None):
        near, *far = row_taps(features, before, after, w_atrous, ((branch, row_tap),), tokens)
        band_step, remainder = split_of((row_tap - 1) * dilation_list[branch], row_count)
        near, near_way = passed_along(near, -band_step, hold)
        far, far_way = passed_along(far[0], -band_step - 1, hold) if far else (None, near_way)
        arrived[branch, row_tap] = (near, far)
        ways = (near_way, far_way) if near_way.shape[0] < far_way.shape[0] else (far_way, near_way)
        part_way[branch, row_tap] = ways

    totals, steps = total_over_devices(jnp.sum(features, axis=(0, 1), dtype=jnp.float32))
    order = ((2, 0), (2, 2), (1, 0), (1, 2), (0, 0), (0, 2))
    centre, base = {}, None
    for place, (branch, row_tap) in enumerate(order):
        if place == own_place:
            centre[2], centre[1], centre[0], base = own_rows(
                features,
                before,
                after,
                w_atrous,
                (2, 1, 0),
                (w_point, w_project, branch_gain, branch_bias),
                [part_way[2, 0][1]],
            )
        send(branch, row_tap, steps[place - 1 : place] if place else (), base)

    pooled = totals / (row_count * band_count * width_local * half_count)
    pool_input = pooled.astype(jnp.bfloat16)
    pool_value = jnp.dot(pool_input[None, :], w_pool, preferred_element_type=jnp.float32)
    pool_branch = activate(pool_value, branch_gain[4:5], branch_bias[4:5])
    depth = w_project.shape[-1]
    pool_projected = jnp.dot(pool_branch, w_project[4 * depth :], preferred_element_type=jnp.float32)

    base = join((2, 1), base, centre, arrived, w_project, branch_gain, branch_bias)
    pixels = row_count * width_local
    per_peer = pixels // device_count
    slots = pixel_order.reshape(pixels, 1)
    tail = (pool_projected, project_gain[None, :], project_bias[None, :], slots)
    outgoing = join((0,), base, centre, arrived, w_project, branch_gain, branch_bias, tail)
    outgoing = outgoing.reshape(device_count, per_peer, depth)
    owned = lax.all_to_all(outgoing, ("band", "sample"), split_axis=0, concat_axis=0, tiled=True)
    return owned.reshape(device_count * per_peer, depth)


def solution(mesh):
    in_specs = (
        P("band", "sample", None),
        P(),
        P(),
        P(),
        P(),
        P(),
        P(),
        P(),
        P(),
        P("band", "sample"),
    )
    out_specs = P(("band", "sample"), None)
    return jax.shard_map(shards, mesh=mesh, in_specs=in_specs, out_specs=out_specs, check_vma=False)
```

```python
import functools

import jax
import jax.numpy as jnp
from jax import lax
from jax.experimental import pallas as pl
from jax.experimental.pallas import tpu as pltpu
from jax.sharding import PartitionSpec as P

dilation_list = (12, 24, 36)
pad = 48
vmem_limit = 24 * 2**20
wide_limit = 56 * 2**20
small_cost = pl.CostEstimate(flops=1024, bytes_accessed=1024, transcendentals=0)
routes = {5: "within", 2: "split"}
own_place = 4
levels = 4


def activate(values, gain, shift_term):
    return jnp.maximum(values * gain + shift_term, 0.0).astype(jnp.bfloat16)


def neighbours_columns(features):
    half_count = lax.axis_size("sample")
    width = features.shape[1]
    leading = features[:, :pad]
    last = features[:, width - pad :]
    up = [(i, (i + 1) % half_count) for i in range(half_count)]
    down = [(j, i) for i, j in up]
    if half_count == 2:
        both = lax.ppermute(jnp.concatenate([leading, last], axis=1), "sample", up)
        return both[:, pad:], both[:, :pad]
    return lax.ppermute(last, "sample", up), lax.ppermute(leading, "sample", down)


def passed_along(array, by, hold=None):
    band_count = lax.axis_size("band")
    half_count = lax.axis_size("sample")
    level = max(band_count // levels, 1)
    route = routes.get(abs(by), "direct")
    if by % level == 0:
        route = "direct"
    first, second = [], []
    for band in range(band_count):
        goal = band + by
        if not 0 <= goal < band_count:
            continue
        along = goal // level * level + band % level
        within = band // level * level + goal % level
        for half in range(half_count):
            if route == "direct":
                middle = goal
            elif route == "within" or half % 2:
                middle = within
            else:
                middle = along
            first.append((band * half_count + half, middle * half_count + half))
            second.append((middle * half_count + half, goal * half_count + half))
    if not first:
        return jnp.zeros_like(array), array
    array = lax.ppermute(array, ("band", "sample"), first)
    part_way = array
    if route != "direct":
        if hold is not None:
            array, _ = lax.optimization_barrier((array, hold))
        array = lax.ppermute(array, ("band", "sample"), second)
    return array, part_way


def total_over_devices(values):
    steps = []
    for axis in ("sample", "band"):
        size = lax.axis_size(axis)
        if size & (size - 1):
            values = lax.psum(values, axis)
            steps.append(values)
            continue
        step = 1
        while step < size:
            values = values + lax.ppermute(values, axis, [(i, i ^ step) for i in range(size)])
            steps.append(values)
            step *= 2
    return values, steps


def split_of(offset, row_count):
    band_step = offset // row_count
    return band_step, offset - band_step * row_count


def taps_body(plan, row_count, token_count, x_ref, before_ref, after_ref, *refs):
    weights = refs[: len(plan)]
    outs = refs[len(plan) + token_count : -1]
    wide = refs[-1]
    width = x_ref.shape[1]
    row = pl.program_id(0)
    wide[0:pad] = before_ref[0]
    wide[pad : pad + width] = x_ref[0]
    wide[pad + width :] = after_ref[0]
    place = 0
    for (branch, row_tap), w_ref in zip(plan, weights):
        dilation = dilation_list[branch]
        summed = None
        for column_tap in range(3):
            start = pad + (column_tap - 1) * dilation
            term = jnp.dot(
                wide[start : start + width],
                w_ref[0, 0, column_tap],
                preferred_element_type=jnp.float32,
            )
            summed = term if summed is None else summed + term
        summed = summed.astype(jnp.bfloat16)
        _, remainder = split_of((row_tap - 1) * dilation, row_count)
        near = outs[place]
        place += 1
        if remainder:
            far = outs[place]
            place += 1

            @pl.when(row >= remainder)
            def _():
                near[0] = summed

            @pl.when(row < remainder)
            def _():
                far[0] = summed
        else:
            near[0] = summed


def row_taps(features, before, after, w_atrous, plan, tokens=()):
    row_count, width, channels = features.shape
    depth = w_atrous.shape[-1]
    in_specs = [
        pl.BlockSpec((1, width, channels), lambda r: (r, 0, 0)),
        pl.BlockSpec((1, pad, channels), lambda r: (r, 0, 0)),
        pl.BlockSpec((1, pad, channels), lambda r: (r, 0, 0)),
    ]
    out_specs, out_shapes = [], []
    for branch, row_tap in plan:
        in_specs.append(
            pl.BlockSpec(
                (1, 1, 3, channels, depth),
                functools.partial(lambda branch, row_tap, r: (branch, row_tap, 0, 0, 0), branch, row_tap),
            )
        )
        _, remainder = split_of((row_tap - 1) * dilation_list[branch], row_count)
        out_specs.append(
            pl.BlockSpec(
                (1, width, depth),
                functools.partial(lambda remainder, r: (jnp.maximum(r - remainder, 0), 0, 0), remainder),
            )
        )
        out_shapes.append(jax.ShapeDtypeStruct((row_count - remainder, width, depth), jnp.bfloat16))
        if remainder:
            out_specs.append(
                pl.BlockSpec(
                    (1, width, depth),
                    functools.partial(lambda remainder, r: (jnp.minimum(r, remainder - 1), 0, 0), remainder),
                )
            )
            out_shapes.append(jax.ShapeDtypeStruct((remainder, width, depth), jnp.bfloat16))
    return pl.pallas_call(
        functools.partial(taps_body, plan, row_count, len(tokens)),
        grid=(row_count,),
        in_specs=in_specs + [pl.BlockSpec(memory_space=pl.ANY)] * len(tokens),
        out_specs=out_specs,
        out_shape=out_shapes,
        scratch_shapes=[pltpu.VMEM((width + 2 * pad, channels), jnp.bfloat16)],
        compiler_params=pltpu.CompilerParams(vmem_limit_bytes=vmem_limit),
        cost_estimate=small_cost,
    )(features, before, after, *([w_atrous] * len(plan)), *tokens)


def own_body(plan, with_point, token_count, x_ref, before_ref, after_ref, *refs):
    weights = refs[: len(plan)]
    place = len(plan)
    if with_point:
        w_point, w_project, gain, shift_term = refs[place : place + 4]
        place += 4
    place += token_count
    centres = refs[place : place + len(plan)]
    extra_ref, wide = refs[place + len(plan) :]
    width = x_ref.shape[1]
    wide[0:pad] = before_ref[0]
    wide[pad : pad + width] = x_ref[0]
    wide[pad + width :] = after_ref[0]
    for branch, w_ref, centre_ref in zip(plan, weights, centres):
        dilation = dilation_list[branch]
        summed = None
        for column_tap in range(3):
            start = pad + (column_tap - 1) * dilation
            term = jnp.dot(
                wide[start : start + width],
                w_ref[0, 0, column_tap],
                preferred_element_type=jnp.float32,
            )
            summed = term if summed is None else summed + term
        centre_ref[0] = summed
    if with_point:
        point = jnp.dot(x_ref[0], w_point[...], preferred_element_type=jnp.float32)
        point = activate(point, gain[0:1], shift_term[0:1])
        extra_ref[0] = jnp.dot(point, w_project[...], preferred_element_type=jnp.float32)


def own_rows(features, before, after, w_atrous, plan, point_operands=None, tokens=()):
    row_count, width, channels = features.shape
    depth = w_atrous.shape[-1]
    whole = lambda array: pl.BlockSpec(array.shape, lambda r: (0,) * array.ndim)
    operands = [features, before, after] + [w_atrous] * len(plan)
    in_specs = [
        pl.BlockSpec((1, width, channels), lambda r: (r, 0, 0)),
        pl.BlockSpec((1, pad, channels), lambda r: (r, 0, 0)),
        pl.BlockSpec((1, pad, channels), lambda r: (r, 0, 0)),
    ]
    for branch in plan:
        in_specs.append(
            pl.BlockSpec(
                (1, 1, 3, channels, depth),
                functools.partial(lambda branch, r: (branch, 1, 0, 0, 0), branch),
            )
        )
    row_block = pl.BlockSpec((1, width, depth), lambda r: (r, 0, 0))
    row_type = jax.ShapeDtypeStruct((row_count, width, depth), jnp.float32)
    if point_operands is not None:
        w_point, w_project, gain, shift_term = point_operands
        operands += [w_point, w_project, gain, shift_term]
        in_specs += [
            whole(w_point),
            pl.BlockSpec((depth, depth), lambda r: (0, 0)),
            whole(gain),
            whole(shift_term),
        ]
        extra_spec, extra_type = row_block, row_type
    else:
        extra_spec = pl.BlockSpec((1, channels), lambda r: (0, 0))
        extra_type = jax.ShapeDtypeStruct((1, channels), jnp.float32)
    operands += list(tokens)
    in_specs += [pl.BlockSpec(memory_space=pl.ANY)] * len(tokens)
    return pl.pallas_call(
        functools.partial(own_body, plan, point_operands is not None, len(tokens)),
        grid=(row_count,),
        in_specs=in_specs,
        out_specs=[row_block] * len(plan) + [extra_spec],
        out_shape=[row_type] * len(plan) + [extra_type],
        scratch_shapes=[pltpu.VMEM((width + 2 * pad, channels), jnp.bfloat16)],
        compiler_params=pltpu.CompilerParams(vmem_limit_bytes=wide_limit),
        cost_estimate=small_cost,
    )(*operands)


def join_body(plan, remainders, last, base_ref, w_project, gain, shift_term, *refs):
    row = pl.program_id(0)
    total = base_ref[0]
    place = 0
    for branch in plan:
        summed = refs[place][0]
        place += 1
        for row_tap in (0, 2):
            remainder = remainders[branch, row_tap]
            near = refs[place][0].astype(jnp.float32)
            place += 1
            if remainder:
                far = refs[place][0].astype(jnp.float32)
                place += 1
                own_near = base_ref.shape[0] * pl.num_programs(0) - remainder
                near = jnp.where(row < own_near, near, far)
            summed = summed + near
        value = activate(summed, gain[branch + 1 : branch + 2], shift_term[branch + 1 : branch + 2])
        depth = value.shape[-1]
        total = total + jnp.dot(
            value,
            w_project[(branch + 1) * depth : (branch + 2) * depth],
            preferred_element_type=jnp.float32,
        )
    if last:
        pooled, project_gain, project_bias, slots, out, cells = refs[place:]
        width = total.shape[0]
        pixels = cells.shape[0]
        cells[pl.ds(pl.multiple_of(row * width, width), width)] = activate(
            total + pooled[...], project_gain[...], project_bias[...]
        )

        @pl.when(row == pl.num_programs(0) - 1)
        def _():
            for start in range(0, pixels, width):
                place_of = lax.broadcasted_iota(jnp.int32, (width, pixels), 1)
                picked = jnp.where(slots[start : start + width] == place_of, 1.0, 0.0)
                out[start : start + width] = jnp.dot(
                    picked.astype(jnp.bfloat16), cells[...], preferred_element_type=jnp.float32
                ).astype(jnp.bfloat16)
    else:
        refs[place][0] = total


def join(plan, base, centre, arrived, w_project, gain, shift_term, tail=None):
    row_count, width, depth = base.shape
    whole = lambda array: pl.BlockSpec(array.shape, lambda r: (0,) * array.ndim)
    block = pl.BlockSpec((1, width, depth), lambda r: (r, 0, 0))
    operands = [base, w_project, gain, shift_term]
    in_specs = [block, whole(w_project), whole(gain), whole(shift_term)]
    remainders = {}
    for branch in plan:
        operands.append(centre[branch])
        in_specs.append(block)
        for row_tap in (0, 2):
            _, remainder = split_of((row_tap - 1) * dilation_list[branch], row_count)
            remainders[branch, row_tap] = remainder
            near_count = row_count - remainder
            near, far = arrived[branch, row_tap]
            operands.append(near)
            in_specs.append(
                pl.BlockSpec(
                    (1, width, depth),
                    functools.partial(lambda n, r: (jnp.minimum(r, n - 1), 0, 0), near_count),
                )
            )
            if remainder:
                operands.append(far)
                in_specs.append(
                    pl.BlockSpec(
                        (1, width, depth),
                        functools.partial(lambda n, r: (jnp.maximum(r - n, 0), 0, 0), near_count),
                    )
                )
    out_spec, scratch = block, []
    out_type = jax.ShapeDtypeStruct((row_count, width, depth), jnp.float32)
    if tail is not None:
        operands += list(tail)
        in_specs += [whole(array) for array in tail]
        out_type = jax.ShapeDtypeStruct((row_count * width, depth), jnp.bfloat16)
        out_spec = pl.BlockSpec((row_count * width, depth), lambda r: (0, 0))
        scratch = [pltpu.VMEM((row_count * width, depth), jnp.bfloat16)]
    return pl.pallas_call(
        functools.partial(join_body, plan, remainders, tail is not None),
        grid=(row_count,),
        in_specs=in_specs,
        out_specs=out_spec,
        out_shape=out_type,
        scratch_shapes=scratch,
        compiler_params=pltpu.CompilerParams(vmem_limit_bytes=wide_limit),
        cost_estimate=small_cost,
    )(*operands)


def shards(
    features,
    w_point,
    w_atrous,
    w_pool,
    branch_gain,
    branch_bias,
    w_project,
    project_gain,
    project_bias,
    pixel_order,
):
    row_count, width_local, channels = features.shape
    band_count = lax.axis_size("band")
    half_count = lax.axis_size("sample")
    device_count = band_count * half_count
    before, after = neighbours_columns(features)

    arrived, part_way = {}, {}

    def send(branch, row_tap, tokens=(), hold=None):
        near, *far = row_taps(features, before, after, w_atrous, ((branch, row_tap),), tokens)
        band_step, remainder = split_of((row_tap - 1) * dilation_list[branch], row_count)
        near, near_way = passed_along(near, -band_step, hold)
        far, far_way = passed_along(far[0], -band_step - 1, hold) if far else (None, near_way)
        arrived[branch, row_tap] = (near, far)
        ways = (near_way, far_way) if near_way.shape[0] < far_way.shape[0] else (far_way, near_way)
        part_way[branch, row_tap] = ways

    totals, steps = total_over_devices(
        lax.optimization_barrier((jnp.sum(features, axis=(0, 1), dtype=jnp.float32), before))[0]
    )
    order = ((2, 0), (2, 2), (1, 0), (1, 2), (0, 0), (0, 2))
    centre, base = {}, None
    for place, (branch, row_tap) in enumerate(order):
        if place == own_place:
            centre[2], centre[1], centre[0], base = own_rows(
                features,
                before,
                after,
                w_atrous,
                (2, 1, 0),
                (w_point, w_project, branch_gain, branch_bias),
                [part_way[2, 0][1]],
            )
        send(branch, row_tap, steps[place - 1 : place] if place else (), base)

    pooled = totals / (row_count * band_count * width_local * half_count)
    pool_input = pooled.astype(jnp.bfloat16)
    pool_value = jnp.dot(pool_input[None, :], w_pool, preferred_element_type=jnp.float32)
    pool_branch = activate(pool_value, branch_gain[4:5], branch_bias[4:5])
    depth = w_project.shape[-1]
    pool_projected = jnp.dot(pool_branch, w_project[4 * depth :], preferred_element_type=jnp.float32)

    base = join((2, 1), base, centre, arrived, w_project, branch_gain, branch_bias)
    pixels = row_count * width_local
    per_peer = pixels // device_count
    slots = pixel_order.reshape(pixels, 1)
    tail = (pool_projected, project_gain[None, :], project_bias[None, :], slots)
    outgoing = join((0,), base, centre, arrived, w_project, branch_gain, branch_bias, tail)
    outgoing = outgoing.reshape(device_count, per_peer, depth)
    owned = lax.all_to_all(outgoing, ("band", "sample"), split_axis=0, concat_axis=0, tiled=True)
    return owned.reshape(device_count * per_peer, depth)


def solution(mesh):
    in_specs = (
        P("band", "sample", None),
        P(),
        P(),
        P(),
        P(),
        P(),
        P(),
        P(),
        P(),
        P("band", "sample"),
    )
    out_specs = P(("band", "sample"), None)
    return jax.shard_map(shards, mesh=mesh, in_specs=in_specs, out_specs=out_specs, check_vma=False)
```

```python
import functools

import jax
import jax.numpy as jnp
from jax import lax
from jax.experimental import pallas as pl
from jax.experimental.pallas import tpu as pltpu
from jax.sharding import PartitionSpec as P

dilation_list = (12, 24, 36)
pad = 48
vmem_limit = 24 * 2**20
wide_limit = 56 * 2**20
small_cost = pl.CostEstimate(flops=1024, bytes_accessed=1024, transcendentals=0)
routes = {5: "within", 2: "split"}
own_place = 4
levels = 4


def activate(values, gain, shift_term):
    return jnp.maximum(values * gain + shift_term, 0.0).astype(jnp.bfloat16)


def neighbours_columns(features):
    half_count = lax.axis_size("sample")
    width = features.shape[1]
    leading = features[:, :pad]
    last = features[:, width - pad :]
    up = [(i, (i + 1) % half_count) for i in range(half_count)]
    down = [(j, i) for i, j in up]
    if half_count == 2:
        both = lax.ppermute(jnp.concatenate([leading, last], axis=1), "sample", up)
        return both[:, pad:], both[:, :pad]
    return lax.ppermute(last, "sample", up), lax.ppermute(leading, "sample", down)


def passed_along(array, by, hold=None):
    band_count = lax.axis_size("band")
    half_count = lax.axis_size("sample")
    level = max(band_count // levels, 1)
    route = routes.get(abs(by), "direct")
    if by % level == 0:
        route = "direct"
    first, second = [], []
    for band in range(band_count):
        goal = band + by
        if not 0 <= goal < band_count:
            continue
        along = goal // level * level + band % level
        within = band // level * level + goal % level
        for half in range(half_count):
            if route == "direct":
                middle = goal
            elif route == "within" or half % 2:
                middle = within
            else:
                middle = along
            first.append((band * half_count + half, middle * half_count + half))
            second.append((middle * half_count + half, goal * half_count + half))
    if not first:
        return jnp.zeros_like(array), array
    array = lax.ppermute(array, ("band", "sample"), first)
    part_way = array
    if route != "direct":
        if hold is not None:
            array, _ = lax.optimization_barrier((array, hold))
        array = lax.ppermute(array, ("band", "sample"), second)
    return array, part_way


def total_over_devices(values):
    steps = []
    for axis in ("sample", "band"):
        size = lax.axis_size(axis)
        if size & (size - 1):
            values = lax.psum(values, axis)
            steps.append(values)
            continue
        step = 1
        while step < size:
            values = values + lax.ppermute(values, axis, [(i, i ^ step) for i in range(size)])
            steps.append(values)
            step *= 2
    return values, steps


def split_of(offset, row_count):
    band_step = offset // row_count
    return band_step, offset - band_step * row_count


def taps_body(plan, row_count, token_count, x_ref, before_ref, after_ref, *refs):
    weights = refs[: len(plan)]
    outs = refs[len(plan) + token_count : -1]
    wide = refs[-1]
    width = x_ref.shape[1]
    row = pl.program_id(0)
    wide[0:pad] = before_ref[0]
    wide[pad : pad + width] = x_ref[0]
    wide[pad + width :] = after_ref[0]
    place = 0
    for (branch, row_tap), w_ref in zip(plan, weights):
        dilation = dilation_list[branch]
        summed = None
        for column_tap in range(3):
            start = pad + (column_tap - 1) * dilation
            term = jnp.dot(
                wide[start : start + width],
                w_ref[0, 0, column_tap],
                preferred_element_type=jnp.float32,
            )
            summed = term if summed is None else summed + term
        summed = summed.astype(jnp.bfloat16)
        _, remainder = split_of((row_tap - 1) * dilation, row_count)
        near = outs[place]
        place += 1
        if remainder:
            far = outs[place]
            place += 1

            @pl.when(row >= remainder)
            def _():
                near[0] = summed

            @pl.when(row < remainder)
            def _():
                far[0] = summed
        else:
            near[0] = summed


def row_taps(features, before, after, w_atrous, plan, tokens=()):
    row_count, width, channels = features.shape
    depth = w_atrous.shape[-1]
    in_specs = [
        pl.BlockSpec((1, width, channels), lambda r: (r, 0, 0)),
        pl.BlockSpec((1, pad, channels), lambda r: (r, 0, 0)),
        pl.BlockSpec((1, pad, channels), lambda r: (r, 0, 0)),
    ]
    out_specs, out_shapes = [], []
    for branch, row_tap in plan:
        in_specs.append(
            pl.BlockSpec(
                (1, 1, 3, channels, depth),
                functools.partial(lambda branch, row_tap, r: (branch, row_tap, 0, 0, 0), branch, row_tap),
            )
        )
        _, remainder = split_of((row_tap - 1) * dilation_list[branch], row_count)
        out_specs.append(
            pl.BlockSpec(
                (1, width, depth),
                functools.partial(lambda remainder, r: (jnp.maximum(r - remainder, 0), 0, 0), remainder),
            )
        )
        out_shapes.append(jax.ShapeDtypeStruct((row_count - remainder, width, depth), jnp.bfloat16))
        if remainder:
            out_specs.append(
                pl.BlockSpec(
                    (1, width, depth),
                    functools.partial(lambda remainder, r: (jnp.minimum(r, remainder - 1), 0, 0), remainder),
                )
            )
            out_shapes.append(jax.ShapeDtypeStruct((remainder, width, depth), jnp.bfloat16))
    return pl.pallas_call(
        functools.partial(taps_body, plan, row_count, len(tokens)),
        grid=(row_count,),
        in_specs=in_specs + [pl.BlockSpec(memory_space=pl.ANY)] * len(tokens),
        out_specs=out_specs,
        out_shape=out_shapes,
        scratch_shapes=[pltpu.VMEM((width + 2 * pad, channels), jnp.bfloat16)],
        compiler_params=pltpu.CompilerParams(vmem_limit_bytes=vmem_limit),
        cost_estimate=small_cost,
    )(features, before, after, *([w_atrous] * len(plan)), *tokens)


def own_body(plan, with_point, token_count, x_ref, before_ref, after_ref, *refs):
    weights = refs[: len(plan)]
    place = len(plan)
    if with_point:
        w_point, w_project, gain, shift_term = refs[place : place + 4]
        place += 4
    place += token_count
    centres = refs[place : place + len(plan)]
    extra_ref, wide = refs[place + len(plan) :]
    width = x_ref.shape[1]
    wide[0:pad] = before_ref[0]
    wide[pad : pad + width] = x_ref[0]
    wide[pad + width :] = after_ref[0]
    for branch, w_ref, centre_ref in zip(plan, weights, centres):
        dilation = dilation_list[branch]
        summed = None
        for column_tap in range(3):
            start = pad + (column_tap - 1) * dilation
            term = jnp.dot(
                wide[start : start + width],
                w_ref[0, 0, column_tap],
                preferred_element_type=jnp.float32,
            )
            summed = term if summed is None else summed + term
        centre_ref[0] = summed
    if with_point:
        point = jnp.dot(x_ref[0], w_point[...], preferred_element_type=jnp.float32)
        point = activate(point, gain[0:1], shift_term[0:1])
        extra_ref[0] = jnp.dot(point, w_project[...], preferred_element_type=jnp.float32)


def own_rows(features, before, after, w_atrous, plan, point_operands=None, tokens=()):
    row_count, width, channels = features.shape
    depth = w_atrous.shape[-1]
    whole = lambda array: pl.BlockSpec(array.shape, lambda r: (0,) * array.ndim)
    operands = [features, before, after] + [w_atrous] * len(plan)
    in_specs = [
        pl.BlockSpec((1, width, channels), lambda r: (r, 0, 0)),
        pl.BlockSpec((1, pad, channels), lambda r: (r, 0, 0)),
        pl.BlockSpec((1, pad, channels), lambda r: (r, 0, 0)),
    ]
    for branch in plan:
        in_specs.append(
            pl.BlockSpec(
                (1, 1, 3, channels, depth),
                functools.partial(lambda branch, r: (branch, 1, 0, 0, 0), branch),
            )
        )
    row_block = pl.BlockSpec((1, width, depth), lambda r: (r, 0, 0))
    row_type = jax.ShapeDtypeStruct((row_count, width, depth), jnp.float32)
    if point_operands is not None:
        w_point, w_project, gain, shift_term = point_operands
        operands += [w_point, w_project, gain, shift_term]
        in_specs += [
            whole(w_point),
            pl.BlockSpec((depth, depth), lambda r: (0, 0)),
            whole(gain),
            whole(shift_term),
        ]
        extra_spec, extra_type = row_block, row_type
    else:
        extra_spec = pl.BlockSpec((1, channels), lambda r: (0, 0))
        extra_type = jax.ShapeDtypeStruct((1, channels), jnp.float32)
    operands += list(tokens)
    in_specs += [pl.BlockSpec(memory_space=pl.ANY)] * len(tokens)
    return pl.pallas_call(
        functools.partial(own_body, plan, point_operands is not None, len(tokens)),
        grid=(row_count,),
        in_specs=in_specs,
        out_specs=[row_block] * len(plan) + [extra_spec],
        out_shape=[row_type] * len(plan) + [extra_type],
        scratch_shapes=[pltpu.VMEM((width + 2 * pad, channels), jnp.bfloat16)],
        compiler_params=pltpu.CompilerParams(vmem_limit_bytes=wide_limit),
        cost_estimate=small_cost,
    )(*operands)


def join_body(plan, remainders, last, base_ref, w_project, gain, shift_term, *refs):
    row = pl.program_id(0)
    total = base_ref[0]
    place = 0
    for branch in plan:
        summed = refs[place][0]
        place += 1
        for row_tap in (0, 2):
            remainder = remainders[branch, row_tap]
            near = refs[place][0].astype(jnp.float32)
            place += 1
            if remainder:
                far = refs[place][0].astype(jnp.float32)
                place += 1
                own_near = base_ref.shape[0] * pl.num_programs(0) - remainder
                near = jnp.where(row < own_near, near, far)
            summed = summed + near
        value = activate(summed, gain[branch + 1 : branch + 2], shift_term[branch + 1 : branch + 2])
        depth = value.shape[-1]
        total = total + jnp.dot(
            value,
            w_project[(branch + 1) * depth : (branch + 2) * depth],
            preferred_element_type=jnp.float32,
        )
    if last:
        pooled, project_gain, project_bias, slots, out, cells = refs[place:]
        width = total.shape[0]
        pixels = cells.shape[0]
        cells[pl.ds(pl.multiple_of(row * width, width), width)] = activate(
            total + pooled[...], project_gain[...], project_bias[...]
        )

        @pl.when(row == pl.num_programs(0) - 1)
        def _():
            for start in range(0, pixels, width):
                place_of = lax.broadcasted_iota(jnp.int32, (width, pixels), 1)
                picked = jnp.where(slots[start : start + width] == place_of, 1.0, 0.0)
                out[start : start + width] = jnp.dot(
                    picked.astype(jnp.bfloat16), cells[...], preferred_element_type=jnp.float32
                ).astype(jnp.bfloat16)
    else:
        refs[place][0] = total


def join(plan, base, centre, arrived, w_project, gain, shift_term, tail=None):
    row_count, width, depth = base.shape
    whole = lambda array: pl.BlockSpec(array.shape, lambda r: (0,) * array.ndim)
    block = pl.BlockSpec((1, width, depth), lambda r: (r, 0, 0))
    operands = [base, w_project, gain, shift_term]
    in_specs = [block, whole(w_project), whole(gain), whole(shift_term)]
    remainders = {}
    for branch in plan:
        operands.append(centre[branch])
        in_specs.append(block)
        for row_tap in (0, 2):
            _, remainder = split_of((row_tap - 1) * dilation_list[branch], row_count)
            remainders[branch, row_tap] = remainder
            near_count = row_count - remainder
            near, far = arrived[branch, row_tap]
            operands.append(near)
            in_specs.append(
                pl.BlockSpec(
                    (1, width, depth),
                    functools.partial(lambda n, r: (jnp.minimum(r, n - 1), 0, 0), near_count),
                )
            )
            if remainder:
                operands.append(far)
                in_specs.append(
                    pl.BlockSpec(
                        (1, width, depth),
                        functools.partial(lambda n, r: (jnp.maximum(r - n, 0), 0, 0), near_count),
                    )
                )
    out_spec, scratch = block, []
    out_type = jax.ShapeDtypeStruct((row_count, width, depth), jnp.float32)
    if tail is not None:
        operands += list(tail)
        in_specs += [whole(array) for array in tail]
        out_type = jax.ShapeDtypeStruct((row_count * width, depth), jnp.bfloat16)
        out_spec = pl.BlockSpec((row_count * width, depth), lambda r: (0, 0))
        scratch = [pltpu.VMEM((row_count * width, depth), jnp.bfloat16)]
    return pl.pallas_call(
        functools.partial(join_body, plan, remainders, tail is not None),
        grid=(row_count,),
        in_specs=in_specs,
        out_specs=out_spec,
        out_shape=out_type,
        scratch_shapes=scratch,
        compiler_params=pltpu.CompilerParams(vmem_limit_bytes=wide_limit),
        cost_estimate=small_cost,
    )(*operands)


def shards(
    features,
    w_point,
    w_atrous,
    w_pool,
    branch_gain,
    branch_bias,
    w_project,
    project_gain,
    project_bias,
    pixel_order,
):
    row_count, width_local, channels = features.shape
    band_count = lax.axis_size("band")
    half_count = lax.axis_size("sample")
    device_count = band_count * half_count
    before, after = neighbours_columns(features)

    arrived, part_way = {}, {}

    def send(branch, row_tap, tokens=(), hold=None):
        near, *far = row_taps(features, before, after, w_atrous, ((branch, row_tap),), tokens)
        band_step, remainder = split_of((row_tap - 1) * dilation_list[branch], row_count)
        near, near_way = passed_along(near, -band_step, hold)
        far, far_way = passed_along(far[0], -band_step - 1, hold) if far else (None, near_way)
        arrived[branch, row_tap] = (near, far)
        ways = (near_way, far_way) if near_way.shape[0] < far_way.shape[0] else (far_way, near_way)
        part_way[branch, row_tap] = ways

    totals, steps = total_over_devices(
        lax.optimization_barrier((jnp.sum(features, axis=(0, 1), dtype=jnp.float32), before))[0]
    )
    order = ((2, 2), (2, 0), (1, 2), (1, 0), (0, 2), (0, 0))
    centre, base = {}, None
    for place, (branch, row_tap) in enumerate(order):
        if place == own_place:
            centre[2], centre[1], centre[0], base = own_rows(
                features,
                before,
                after,
                w_atrous,
                (2, 1, 0),
                (w_point, w_project, branch_gain, branch_bias),
                [part_way[2, 2][1]],
            )
        send(branch, row_tap, steps[place - 1 : place] if place else (), base)

    pooled = totals / (row_count * band_count * width_local * half_count)
    pool_input = pooled.astype(jnp.bfloat16)
    pool_value = jnp.dot(pool_input[None, :], w_pool, preferred_element_type=jnp.float32)
    pool_branch = activate(pool_value, branch_gain[4:5], branch_bias[4:5])
    depth = w_project.shape[-1]
    pool_projected = jnp.dot(pool_branch, w_project[4 * depth :], preferred_element_type=jnp.float32)

    base = join((2, 1), base, centre, arrived, w_project, branch_gain, branch_bias)
    pixels = row_count * width_local
    per_peer = pixels // device_count
    slots = pixel_order.reshape(pixels, 1)
    tail = (pool_projected, project_gain[None, :], project_bias[None, :], slots)
    outgoing = join((0,), base, centre, arrived, w_project, branch_gain, branch_bias, tail)
    outgoing = outgoing.reshape(device_count, per_peer, depth)
    owned = lax.all_to_all(outgoing, ("band", "sample"), split_axis=0, concat_axis=0, tiled=True)
    return owned.reshape(device_count * per_peer, depth)


def solution(mesh):
    in_specs = (
        P("band", "sample", None),
        P(),
        P(),
        P(),
        P(),
        P(),
        P(),
        P(),
        P(),
        P("band", "sample"),
    )
    out_specs = P(("band", "sample"), None)
    return jax.shard_map(shards, mesh=mesh, in_specs=in_specs, out_specs=out_specs, check_vma=False)
```

```python
import functools

import jax
import jax.numpy as jnp
from jax import lax
from jax.experimental import pallas as pl
from jax.experimental.pallas import tpu as pltpu
from jax.sharding import PartitionSpec as P

dilation_list = (12, 24, 36)
pad = 48
vmem_limit = 24 * 2**20
wide_limit = 56 * 2**20
small_cost = pl.CostEstimate(flops=1024, bytes_accessed=1024, transcendentals=0)
routes = {5: "within", 2: "split"}
own_place = 4
levels = 4


def activate(values, gain, shift_term):
    return jnp.maximum(values * gain + shift_term, 0.0).astype(jnp.bfloat16)


def neighbours_columns(features):
    half_count = lax.axis_size("sample")
    width = features.shape[1]
    leading = features[:, :pad]
    last = features[:, width - pad :]
    up = [(i, (i + 1) % half_count) for i in range(half_count)]
    down = [(j, i) for i, j in up]
    if half_count == 2:
        both = lax.ppermute(jnp.concatenate([leading, last], axis=1), "sample", up)
        return both[:, pad:], both[:, :pad]
    return lax.ppermute(last, "sample", up), lax.ppermute(leading, "sample", down)


def passed_along(array, by, hold=None):
    band_count = lax.axis_size("band")
    half_count = lax.axis_size("sample")
    level = max(band_count // levels, 1)
    route = routes.get(abs(by), "direct")
    if by % level == 0:
        route = "direct"
    first, second = [], []
    for band in range(band_count):
        goal = band + by
        if not 0 <= goal < band_count:
            continue
        along = goal // level * level + band % level
        within = band // level * level + goal % level
        for half in range(half_count):
            if route == "direct":
                middle = goal
            elif route == "within" or half % 2:
                middle = within
            else:
                middle = along
            first.append((band * half_count + half, middle * half_count + half))
            second.append((middle * half_count + half, goal * half_count + half))
    if not first:
        return jnp.zeros_like(array), array
    array = lax.ppermute(array, ("band", "sample"), first)
    part_way = array
    if route != "direct":
        if hold is not None:
            array, _ = lax.optimization_barrier((array, hold))
        array = lax.ppermute(array, ("band", "sample"), second)
    return array, part_way


def total_over_devices(values):
    steps = []
    for axis in ("sample", "band"):
        size = lax.axis_size(axis)
        if size & (size - 1):
            values = lax.psum(values, axis)
            steps.append(values)
            continue
        step = 1
        while step < size:
            values = values + lax.ppermute(values, axis, [(i, i ^ step) for i in range(size)])
            steps.append(values)
            step *= 2
    return values, steps


def split_of(offset, row_count):
    band_step = offset // row_count
    return band_step, offset - band_step * row_count


def taps_body(plan, row_count, token_count, x_ref, before_ref, after_ref, *refs):
    weights = refs[: len(plan)]
    outs = refs[len(plan) + token_count : -1]
    wide = refs[-1]
    width = x_ref.shape[1]
    row = pl.program_id(0)
    wide[0:pad] = before_ref[0]
    wide[pad : pad + width] = x_ref[0]
    wide[pad + width :] = after_ref[0]
    place = 0
    for (branch, row_tap), w_ref in zip(plan, weights):
        dilation = dilation_list[branch]
        summed = None
        for column_tap in range(3):
            start = pad + (column_tap - 1) * dilation
            term = jnp.dot(
                wide[start : start + width],
                w_ref[0, 0, column_tap],
                preferred_element_type=jnp.float32,
            )
            summed = term if summed is None else summed + term
        summed = summed.astype(jnp.bfloat16)
        _, remainder = split_of((row_tap - 1) * dilation, row_count)
        near = outs[place]
        place += 1
        if remainder:
            far = outs[place]
            place += 1

            @pl.when(row >= remainder)
            def _():
                near[0] = summed

            @pl.when(row < remainder)
            def _():
                far[0] = summed
        else:
            near[0] = summed


def row_taps(features, before, after, w_atrous, plan, tokens=()):
    row_count, width, channels = features.shape
    depth = w_atrous.shape[-1]
    in_specs = [
        pl.BlockSpec((1, width, channels), lambda r: (r, 0, 0)),
        pl.BlockSpec((1, pad, channels), lambda r: (r, 0, 0)),
        pl.BlockSpec((1, pad, channels), lambda r: (r, 0, 0)),
    ]
    out_specs, out_shapes = [], []
    for branch, row_tap in plan:
        in_specs.append(
            pl.BlockSpec(
                (1, 1, 3, channels, depth),
                functools.partial(lambda branch, row_tap, r: (branch, row_tap, 0, 0, 0), branch, row_tap),
            )
        )
        _, remainder = split_of((row_tap - 1) * dilation_list[branch], row_count)
        out_specs.append(
            pl.BlockSpec(
                (1, width, depth),
                functools.partial(lambda remainder, r: (jnp.maximum(r - remainder, 0), 0, 0), remainder),
            )
        )
        out_shapes.append(jax.ShapeDtypeStruct((row_count - remainder, width, depth), jnp.bfloat16))
        if remainder:
            out_specs.append(
                pl.BlockSpec(
                    (1, width, depth),
                    functools.partial(lambda remainder, r: (jnp.minimum(r, remainder - 1), 0, 0), remainder),
                )
            )
            out_shapes.append(jax.ShapeDtypeStruct((remainder, width, depth), jnp.bfloat16))
    return pl.pallas_call(
        functools.partial(taps_body, plan, row_count, len(tokens)),
        grid=(row_count,),
        in_specs=in_specs + [pl.BlockSpec(memory_space=pl.ANY)] * len(tokens),
        out_specs=out_specs,
        out_shape=out_shapes,
        scratch_shapes=[pltpu.VMEM((width + 2 * pad, channels), jnp.bfloat16)],
        compiler_params=pltpu.CompilerParams(vmem_limit_bytes=vmem_limit),
        cost_estimate=small_cost,
    )(features, before, after, *([w_atrous] * len(plan)), *tokens)


def own_body(plan, with_point, token_count, x_ref, before_ref, after_ref, *refs):
    weights = refs[: len(plan)]
    place = len(plan)
    if with_point:
        w_point, w_project, gain, shift_term = refs[place : place + 4]
        place += 4
    place += token_count
    centres = refs[place : place + len(plan)]
    extra_ref, wide = refs[place + len(plan) :]
    width = x_ref.shape[1]
    wide[0:pad] = before_ref[0]
    wide[pad : pad + width] = x_ref[0]
    wide[pad + width :] = after_ref[0]
    for branch, w_ref, centre_ref in zip(plan, weights, centres):
        dilation = dilation_list[branch]
        summed = None
        for column_tap in range(3):
            start = pad + (column_tap - 1) * dilation
            term = jnp.dot(
                wide[start : start + width],
                w_ref[0, 0, column_tap],
                preferred_element_type=jnp.float32,
            )
            summed = term if summed is None else summed + term
        centre_ref[0] = summed
    if with_point:
        point = jnp.dot(x_ref[0], w_point[...], preferred_element_type=jnp.float32)
        point = activate(point, gain[0:1], shift_term[0:1])
        extra_ref[0] = jnp.dot(point, w_project[...], preferred_element_type=jnp.float32)


def own_rows(features, before, after, w_atrous, plan, point_operands=None, tokens=()):
    row_count, width, channels = features.shape
    depth = w_atrous.shape[-1]
    whole = lambda array: pl.BlockSpec(array.shape, lambda r: (0,) * array.ndim)
    operands = [features, before, after] + [w_atrous] * len(plan)
    in_specs = [
        pl.BlockSpec((1, width, channels), lambda r: (r, 0, 0)),
        pl.BlockSpec((1, pad, channels), lambda r: (r, 0, 0)),
        pl.BlockSpec((1, pad, channels), lambda r: (r, 0, 0)),
    ]
    for branch in plan:
        in_specs.append(
            pl.BlockSpec(
                (1, 1, 3, channels, depth),
                functools.partial(lambda branch, r: (branch, 1, 0, 0, 0), branch),
            )
        )
    row_block = pl.BlockSpec((1, width, depth), lambda r: (r, 0, 0))
    row_type = jax.ShapeDtypeStruct((row_count, width, depth), jnp.float32)
    if point_operands is not None:
        w_point, w_project, gain, shift_term = point_operands
        operands += [w_point, w_project, gain, shift_term]
        in_specs += [
            whole(w_point),
            pl.BlockSpec((depth, depth), lambda r: (0, 0)),
            whole(gain),
            whole(shift_term),
        ]
        extra_spec, extra_type = row_block, row_type
    else:
        extra_spec = pl.BlockSpec((1, channels), lambda r: (0, 0))
        extra_type = jax.ShapeDtypeStruct((1, channels), jnp.float32)
    operands += list(tokens)
    in_specs += [pl.BlockSpec(memory_space=pl.ANY)] * len(tokens)
    return pl.pallas_call(
        functools.partial(own_body, plan, point_operands is not None, len(tokens)),
        grid=(row_count,),
        in_specs=in_specs,
        out_specs=[row_block] * len(plan) + [extra_spec],
        out_shape=[row_type] * len(plan) + [extra_type],
        scratch_shapes=[pltpu.VMEM((width + 2 * pad, channels), jnp.bfloat16)],
        compiler_params=pltpu.CompilerParams(vmem_limit_bytes=wide_limit),
        cost_estimate=small_cost,
    )(*operands)


def join_body(plan, remainders, last, base_ref, w_project, gain, shift_term, *refs):
    row = pl.program_id(0)
    total = base_ref[0]
    place = 0
    for branch in plan:
        summed = refs[place][0]
        place += 1
        for row_tap in (0, 2):
            remainder = remainders[branch, row_tap]
            near = refs[place][0].astype(jnp.float32)
            place += 1
            if remainder:
                far = refs[place][0].astype(jnp.float32)
                place += 1
                own_near = base_ref.shape[0] * pl.num_programs(0) - remainder
                near = jnp.where(row < own_near, near, far)
            summed = summed + near
        value = activate(summed, gain[branch + 1 : branch + 2], shift_term[branch + 1 : branch + 2])
        depth = value.shape[-1]
        total = total + jnp.dot(
            value,
            w_project[(branch + 1) * depth : (branch + 2) * depth],
            preferred_element_type=jnp.float32,
        )
    if last:
        pooled, project_gain, project_bias, slots, out, cells = refs[place:]
        width = total.shape[0]
        pixels = cells.shape[0]
        cells[pl.ds(pl.multiple_of(row * width, width), width)] = activate(
            total + pooled[...], project_gain[...], project_bias[...]
        )

        @pl.when(row == pl.num_programs(0) - 1)
        def _():
            for start in range(0, pixels, width):
                place_of = lax.broadcasted_iota(jnp.int32, (width, pixels), 1)
                picked = jnp.where(slots[start : start + width] == place_of, 1.0, 0.0)
                out[start : start + width] = jnp.dot(
                    picked.astype(jnp.bfloat16), cells[...], preferred_element_type=jnp.float32
                ).astype(jnp.bfloat16)
    else:
        refs[place][0] = total


def join(plan, base, centre, arrived, w_project, gain, shift_term, tail=None):
    row_count, width, depth = base.shape
    whole = lambda array: pl.BlockSpec(array.shape, lambda r: (0,) * array.ndim)
    block = pl.BlockSpec((1, width, depth), lambda r: (r, 0, 0))
    operands = [base, w_project, gain, shift_term]
    in_specs = [block, whole(w_project), whole(gain), whole(shift_term)]
    remainders = {}
    for branch in plan:
        operands.append(centre[branch])
        in_specs.append(block)
        for row_tap in (0, 2):
            _, remainder = split_of((row_tap - 1) * dilation_list[branch], row_count)
            remainders[branch, row_tap] = remainder
            near_count = row_count - remainder
            near, far = arrived[branch, row_tap]
            operands.append(near)
            in_specs.append(
                pl.BlockSpec(
                    (1, width, depth),
                    functools.partial(lambda n, r: (jnp.minimum(r, n - 1), 0, 0), near_count),
                )
            )
            if remainder:
                operands.append(far)
                in_specs.append(
                    pl.BlockSpec(
                        (1, width, depth),
                        functools.partial(lambda n, r: (jnp.maximum(r - n, 0), 0, 0), near_count),
                    )
                )
    out_spec, scratch = block, []
    out_type = jax.ShapeDtypeStruct((row_count, width, depth), jnp.float32)
    if tail is not None:
        operands += list(tail)
        in_specs += [whole(array) for array in tail]
        out_type = jax.ShapeDtypeStruct((row_count * width, depth), jnp.bfloat16)
        out_spec = pl.BlockSpec((row_count * width, depth), lambda r: (0, 0))
        scratch = [pltpu.VMEM((row_count * width, depth), jnp.bfloat16)]
    return pl.pallas_call(
        functools.partial(join_body, plan, remainders, tail is not None),
        grid=(row_count,),
        in_specs=in_specs,
        out_specs=out_spec,
        out_shape=out_type,
        scratch_shapes=scratch,
        compiler_params=pltpu.CompilerParams(vmem_limit_bytes=wide_limit),
        cost_estimate=small_cost,
    )(*operands)


def shards(
    features,
    w_point,
    w_atrous,
    w_pool,
    branch_gain,
    branch_bias,
    w_project,
    project_gain,
    project_bias,
    pixel_order,
):
    row_count, width_local, channels = features.shape
    band_count = lax.axis_size("band")
    half_count = lax.axis_size("sample")
    device_count = band_count * half_count
    before, after = neighbours_columns(features)

    arrived, part_way = {}, {}

    def send(branch, row_tap, tokens=(), hold=None):
        near, *far = row_taps(features, before, after, w_atrous, ((branch, row_tap),), tokens)
        band_step, remainder = split_of((row_tap - 1) * dilation_list[branch], row_count)
        near, near_way = passed_along(near, -band_step, hold)
        far, far_way = passed_along(far[0], -band_step - 1, hold) if far else (None, near_way)
        arrived[branch, row_tap] = (near, far)
        ways = (near_way, far_way) if near_way.shape[0] < far_way.shape[0] else (far_way, near_way)
        part_way[branch, row_tap] = ways

    totals, steps = total_over_devices(
        lax.optimization_barrier((jnp.sum(features, axis=(0, 1), dtype=jnp.float32), before))[0]
    )
    order = ((2, 2), (2, 0), (1, 2), (1, 0), (0, 0), (0, 2))
    centre, base = {}, None
    for place, (branch, row_tap) in enumerate(order):
        if place == own_place:
            centre[2], centre[1], centre[0], base = own_rows(
                features,
                before,
                after,
                w_atrous,
                (2, 1, 0),
                (w_point, w_project, branch_gain, branch_bias),
                [part_way[2, 2][1]],
            )
        send(branch, row_tap, steps[place - 1 : place] if place else (), base)

    pooled = totals / (row_count * band_count * width_local * half_count)
    pool_input = pooled.astype(jnp.bfloat16)
    pool_value = jnp.dot(pool_input[None, :], w_pool, preferred_element_type=jnp.float32)
    pool_branch = activate(pool_value, branch_gain[4:5], branch_bias[4:5])
    depth = w_project.shape[-1]
    pool_projected = jnp.dot(pool_branch, w_project[4 * depth :], preferred_element_type=jnp.float32)

    base = join((2, 1), base, centre, arrived, w_project, branch_gain, branch_bias)
    pixels = row_count * width_local
    per_peer = pixels // device_count
    slots = pixel_order.reshape(pixels, 1)
    tail = (pool_projected, project_gain[None, :], project_bias[None, :], slots)
    outgoing = join((0,), base, centre, arrived, w_project, branch_gain, branch_bias, tail)
    outgoing = outgoing.reshape(device_count, per_peer, depth)
    owned = lax.all_to_all(outgoing, ("band", "sample"), split_axis=0, concat_axis=0, tiled=True)
    return owned.reshape(device_count * per_peer, depth)


def solution(mesh):
    in_specs = (
        P("band", "sample", None),
        P(),
        P(),
        P(),
        P(),
        P(),
        P(),
        P(),
        P(),
        P("band", "sample"),
    )
    out_specs = P(("band", "sample"), None)
    return jax.shard_map(shards, mesh=mesh, in_specs=in_specs, out_specs=out_specs, check_vma=False)
```
